32 devices in a mesh: dp: 4 (over y, x), expert: 4 (over z), half: 2 (over core).
Axes of the slice: x: 2, y: 2, z: 4, core: 2. Of those that a mesh axis runs over, the one named last changes fastest.
Arguments:
- activations: bfloat16 [2, 256, 2048], P(None, ('dp', 'expert', 'half')), parts along dimension 1, may hold values from -6 to 6
- upstream: bfloat16 [2, 256, 2048], P(None, ('dp', 'expert', 'half')), parts along dimension 1, may hold values from -12 to 12
- routes: int32 [2, 256, 2], P(None, ('dp', 'expert', 'half')), parts along dimension 1, may hold values from 0 to 3, all different within a row; in each aligned block of 8 rows (0 to 7, 8 to 15, ..., all dimensions but the last counted through in order) at most 4 rows name the same one
- route_gates: float32 [2, 256, 2], P(None, ('dp', 'expert', 'half')), parts along dimension 1, may hold values from 0.05 to 0.2
- gate_matrix: bfloat16 [4, 2048, 512], P('expert', None, 'half'), may hold values from -0.125 to 0.125
- up_matrix: bfloat16 [4, 2048, 512], P('expert', None, 'half'), may hold values from -3 to 3
- down_matrix: bfloat16 [4, 512, 2048], P('expert', 'half'), may hold values from -0.25 to 0.25
Outputs:
- input_cotangent: bfloat16 [2, 256, 2048], P(None, ('dp', 'expert', 'half')), parts along dimension 1
- down_update: bfloat16 [16, 512, 2048], P(('dp', 'expert'), 'half'), parts along dimension 0
The draws below stay inside these ranges and needn't reach their ends.
There are 4 independent parts, one for each index of `dp`. The reference program is written for one: setup_inputs(seed, part) draws one part's arguments, and reference() takes and returns one part's arrays. A program takes and returns all parts, laid end to end along the dimension named above; an argument that names none is the same for every part. Nothing has to cross between parts.
Inputs may be any that keep to these rules, and one draw needn't show every extreme that they name: `routes`: each row names 2 different experts; within the rows of one device in one microbatch (aligned blocks of 8 rows) no expert is named more than 4 times, and in some blocks one expert is named exactly 4 times.
All inputs are finite; a program needn't handle non-finite values.
Results may differ from the reference program's by a relative error of at most 0.007.
Values may be sent and summed in bfloat16 or wider, within the bound.
No kernel may reach another device: no remote copies, remote signals or barrier semaphores. Data moves between devices by JAX's collectives and lax.ppermute only.
A program may use at most 64 MiB of HBM per device.

```python
import math
import jax
import jax.numpy as jnp
import numpy as np
from jax import lax

D = 2048
FF = 512
MB = 2
ITERS = 2
TOK_MB = 8
EXPERTS = 4
TOP = 2
CAP = 4
TOKENS = 64
N_HALF = 2


def draw_upstream(key, part):
    key_own, key_scale = jax.random.split(key, 2)
    column_scale = jnp.exp(jax.random.uniform(key_scale, (D,), jnp.float32) * jnp.log(10.0))
    values = 0.3 * jnp.clip(jax.random.normal(key_own, (MB, TOKENS, D), jnp.float32), -4.0, 4.0)
    return jnp.clip(values * column_scale[None, None, :], -12.0, 12.0).astype(jnp.bfloat16)


def draw_up_matrix(key, part):
    key_entry, key_jitter = jax.random.split(key)
    jitter = jax.random.uniform(key_jitter, (EXPERTS, 1, FF), jnp.float32)
    ladder = (jnp.arange(FF, dtype=jnp.float32)[None, None, :] + jitter) / FF
    column_scale = jnp.exp(ladder * jnp.log(10.0))
    entries = jnp.clip(jax.random.normal(key_entry, (EXPERTS, D, FF), jnp.float32), -4.0, 4.0)
    return jnp.clip(entries * column_scale / jnp.sqrt(1.0 * D), -3.0, 3.0).astype(jnp.bfloat16)


def steps_of(key, extent, pieces, low, high):
    level = 1.0
    for axis_at, blocks in pieces:
        draws = jax.random.uniform(jax.random.fold_in(jax.random.fold_in(key, 6), axis_at), (blocks,), jnp.float32, low / len(pieces), high / len(pieces))
        level = level * jnp.repeat(jnp.exp(draws), extent[axis_at] // blocks).reshape((-1,) + (1,) * (len(extent) - 1 - axis_at))
    return level


def shared_out(stream_key, own, number, rows, number_of, top, limit, lean):
    sequence = jax.random.permutation(stream_key, number_of)
    crowded, usual = portions_of(number_of, rows * top, limit, lean, True), portions_of(number_of, rows * top, limit, lean, False)
    places = jnp.arange(number_of)

    def named(sizes, rotation):
        used = int((sizes > 0).sum())
        fixed = max(1, used // 4)
        moved = fixed + (places - fixed + rotation * (used - fixed)) % max(1, number_of - fixed)
        return jnp.zeros((number_of,), jnp.int32).at[sequence[jnp.where(places < fixed, places, moved)]].set(jnp.asarray(sizes, jnp.int32))

    sizes = jnp.where(number % 4 == 0, named(crowded, number // 4), named(usual, number - number // 4 - 1))
    mixed = jax.random.permutation(jax.random.fold_in(own, 3), number_of)
    donor, taker = mixed[0:number_of // 2 * 2:2], mixed[1:number_of // 2 * 2:2]
    margin = jnp.minimum(sizes[donor] - 1, limit - sizes[taker]) // 2
    margin = jnp.where((donor == sequence[0]) | (taker == sequence[0]) | (sizes[taker] == 0), 0, jnp.maximum(margin, 0))
    moved = jax.random.randint(jax.random.fold_in(own, 4), (number_of // 2,), 0, 1 << 20) % (margin + 1)
    sizes = sizes.at[donor].add(-moved).at[taker].add(moved)
    members = jnp.searchsorted(jnp.cumsum(sizes), jnp.arange(rows * top), side="right").astype(jnp.int32)
    grid = members.reshape(top, rows).T
    grid = grid[jax.random.permutation(jax.random.fold_in(own, 1), rows)]
    rotation = jax.random.randint(jax.random.fold_in(own, 2), (rows, 1), 0, top)
    return jnp.take_along_axis(grid, (jnp.arange(top)[None, :] + rotation) % top, axis=1)


def portions_of(count, total, most, skew, full):
    loads = [(1 << 20) // math.isqrt(standing ** skew) + 1 for standing in range(1, count + 1)]
    largest = most if full else min(most, max(-(-total // count), total * loads[0] // sum(loads)))
    least = 1 if total - largest >= count - 1 else 0
    given, spare = [largest] + [least] * (count - 1), total - largest - least * (count - 1)
    while spare > 0:
        movable = [i for i in range(1, count) if given[i] < largest] or [i for i in range(1, count) if given[i] < most]
        whole, budget = sum([loads[i] for i in movable]), spare
        for i in movable:
            addition = min(most - given[i], max(1, budget * loads[i] // whole), spare)
            given[i] = given[i] + addition
            spare = spare - addition
    return np.array(given)


def centred(key, shape, spread, most, shards=(), kind=jnp.bfloat16):
    drawn = spread * jax.random.normal(key, shape, jnp.float32)
    if shards:
        drawn = drawn * steps_of(key, shape, shards, -0.22, 0.18)
    return jnp.clip(drawn, -most, most).astype(kind)


def setup_inputs(seed: int = 0, part: int = 0) -> dict:
    key_of = jax.random.split(jax.random.key(seed), 8)
    own_keys = jax.random.split(jax.random.fold_in(key_of[7], part), 8)
    activations = centred(own_keys[0], (MB, TOKENS, D), 1.0, 6.0, ((1, 8),))
    upstream = draw_upstream(jax.random.fold_in(jax.random.fold_in(key_of[7], part), 71), part)
    routes_keys = jax.random.split(jax.random.fold_in(own_keys[2], 1), MB * TOKENS // TOK_MB)
    routes_turns = jax.random.permutation(jax.random.fold_in(own_keys[2], 3), MB * TOKENS // TOK_MB)
    routes = jax.vmap(lambda own, number: shared_out(jax.random.fold_in(own_keys[2], 2), own, number, TOK_MB, EXPERTS, TOP, CAP, 2))(routes_keys, routes_turns).reshape((MB, TOKENS, TOP))
    route_gates = jnp.clip(0.05 + 0.15 * jax.random.uniform(own_keys[3], (MB, TOKENS, TOP), jnp.float32) ** steps_of(own_keys[3], (MB, TOKENS, TOP), ((1, 8),), -0.2, 0.2), 0.05, 0.2)
    gate_matrix = centred(key_of[4], (EXPERTS, D, FF), D ** -0.5, 0.125, ((0, 4), (2, 2)))
    up_matrix = draw_up_matrix(jax.random.fold_in(key_of[7], 71), part)
    down_matrix = centred(key_of[6], (EXPERTS, FF, D), FF ** -0.5, 0.25, ((0, 4), (1, 2)))
    return {"activations": activations, "upstream": upstream, "routes": routes, "route_gates": route_gates, "gate_matrix": gate_matrix, "up_matrix": up_matrix, "down_matrix": down_matrix}


linear_term = 3.4445
cubic_term = -4.775
quintic_term = 2.0315

def contract_last(left, right):
    return lax.dot_general(left, right, (((1,), (1,)), ((), ())), preferred_element_type=jnp.float32)

def contract_first(left, right):
    return lax.dot_general(left, right, (((0,), (0,)), ((), ())), preferred_element_type=jnp.float32)

def orthogonalize(down_grad):
    norm_value = jnp.sqrt(jnp.sum(down_grad * down_grad))
    current = down_grad / (norm_value + 1e-07)
    for iteration in range(ITERS):
        rounded = current.astype(jnp.bfloat16)
        gram_full = contract_last(rounded, rounded)
        gram_round = gram_full.astype(jnp.bfloat16)
        square_full = jnp.dot(gram_round, gram_round, preferred_element_type=jnp.float32)
        polynomial = (cubic_term * gram_full + quintic_term * square_full).astype(jnp.bfloat16)
        current = linear_term * current + jnp.dot(polynomial, rounded, preferred_element_type=jnp.float32)
    return (current * math.sqrt(max(FF, D))).astype(jnp.bfloat16)

def expert_step(inputs):
    token_rows, scaled_rows, gate_local, up_local, down_local = inputs
    pre_gate = jnp.dot(token_rows, gate_local, preferred_element_type=jnp.float32)
    pre_up = jnp.dot(token_rows, up_local, preferred_element_type=jnp.float32)
    sigmoid_gate = jax.nn.sigmoid(pre_gate)
    activated = pre_gate * sigmoid_gate
    hidden = (activated * pre_up).astype(jnp.bfloat16)
    hidden_grad = contract_last(scaled_rows, down_local)
    gate_grad = (hidden_grad * pre_up * sigmoid_gate * (1.0 + pre_gate * (1.0 - sigmoid_gate))).astype(jnp.bfloat16)
    up_grad = (hidden_grad * activated).astype(jnp.bfloat16)
    half_width = FF // N_HALF
    summed = jnp.zeros(token_rows.shape, jnp.float32)
    for half_index in range(N_HALF):
        lower = half_index * half_width
        upper = lower + half_width
        piece = contract_last(gate_grad[:, lower:upper], gate_local[:, lower:upper])
        piece = piece + contract_last(up_grad[:, lower:upper], up_local[:, lower:upper])
        summed = summed + lax.optimization_barrier(piece.astype(jnp.bfloat16)).astype(jnp.float32)
    entry_grad = summed.astype(jnp.bfloat16)
    down_grad = contract_first(hidden, scaled_rows)
    return (entry_grad, orthogonalize(down_grad))

def reference(activations, upstream, routes, route_gates, gate_matrix, up_matrix, down_matrix):
    blocks = MB * (TOKENS // TOK_MB)
    row_count = TOK_MB * TOP
    route_rows = routes.reshape(blocks, row_count)
    onehot = (route_rows[:, :, None] == jnp.arange(EXPERTS, dtype=jnp.int32)[None, None, :]).astype(jnp.int32)
    before = jnp.cumsum(onehot, axis=1) - onehot
    position = lax.optimization_barrier(jnp.sum(before * onehot, axis=2)).astype(jnp.int32)
    block_ids = jnp.arange(blocks, dtype=jnp.int32)[:, None]
    target = ((route_rows * blocks + block_ids) * CAP + position).reshape(blocks * row_count).astype(jnp.int32)
    token_ids = (block_ids * TOK_MB + jnp.arange(row_count, dtype=jnp.int32)[None, :] // TOP).reshape(blocks * row_count).astype(jnp.int32)
    flat_tokens = activations.reshape(MB * TOKENS, D)
    scaled = (route_gates[:, :, :, None] * upstream[:, :, None, :].astype(jnp.float32)).astype(jnp.bfloat16)
    scaled = scaled.reshape(MB * TOKENS * TOP, D)
    total = EXPERTS * blocks * CAP
    token_buffer = jnp.zeros((total, D), jnp.bfloat16).at[target].set(flat_tokens[token_ids])
    scaled_buffer = jnp.zeros((total, D), jnp.bfloat16).at[target].set(scaled)
    token_buffer = token_buffer.reshape(EXPERTS, blocks * CAP, D)
    scaled_buffer = scaled_buffer.reshape(EXPERTS, blocks * CAP, D)
    entry_rows, updates = lax.map(expert_step, (token_buffer, scaled_buffer, gate_matrix, up_matrix, down_matrix))
    per_entry = entry_rows.reshape(total, D)[target].astype(jnp.float32).reshape(MB * TOKENS, TOP, D)
    cotangent = lax.optimization_barrier(jnp.sum(per_entry, axis=1)).astype(jnp.bfloat16).reshape(MB, TOKENS, D)
    return (cotangent, updates)
```

```python
import functools
import math

import jax
import jax.numpy as jnp
from jax import lax
from jax.experimental import pallas as pl
from jax.experimental.pallas import tpu as pltpu
from jax.sharding import PartitionSpec as P

ITERS = 2
MAX_PERMUTED = 8

linear_term = 3.4445
cubic_term = -4.775
quintic_term = 2.0315

F32 = jnp.float32
BF16 = jnp.bfloat16


def dot(left, right, dims, precision=None):
    return lax.dot_general(
        left, right, (dims, ((), ())), precision=precision, preferred_element_type=F32
    )


def contract_last(left, right):
    return dot(left, right, ((1,), (1,)))


def plain(left, right, precision=None):
    return dot(left, right, ((1,), (0,)), precision)


def route_rows(x, u, routes, gates, base, tokens_dev, experts, capacity):
    rows, top = routes.shape
    batches = rows // tokens_dev
    block = batches * capacity
    slots = experts * block
    expert_ids = lax.broadcasted_iota(jnp.int32, (rows, experts), 1)
    onehots = [(routes[:, k : k + 1] == expert_ids).astype(F32) for k in range(top)]
    row = lax.broadcasted_iota(jnp.int32, (rows, rows), 0)
    col = lax.broadcasted_iota(jnp.int32, (rows, rows), 1)
    first = row // tokens_dev * tokens_dev
    earlier = jnp.where((col < row) & (col >= first), 1.0, 0.0).astype(BF16)
    before = plain(earlier, sum(onehots).astype(BF16))
    token = lax.broadcasted_iota(jnp.int32, (rows, 1), 0)
    own_block = token // tokens_dev * capacity
    lane = lax.broadcasted_iota(jnp.int32, (rows, slots), 1)
    picks, scaled = [], []
    wide = u.astype(F32)
    for k in range(top):
        position = jnp.sum(before * onehots[k], axis=1, keepdims=True).astype(jnp.int32)
        before = before + onehots[k]
        relative = routes[:, k : k + 1] - base
        relative = jnp.where(relative < 0, relative + experts, relative)
        slot = relative * block + own_block + position
        picks.append(jnp.where(lane == slot, 1.0, 0.0))
        scaled.append(gates[:, k : k + 1] * wide)
    pick_tok = sum(picks)
    select_x = jnp.transpose(pick_tok).astype(BF16)
    select_s = jnp.transpose(jnp.concatenate(picks, axis=0)).astype(BF16)
    x_rows = plain(select_x, x)
    s_rows = plain(select_s, jnp.concatenate(scaled, axis=0).astype(BF16))
    return x_rows, s_rows, pick_tok.astype(BF16)


def forward_values(x_rows, weights):
    hidden, active, slope = [], [], []
    for gate, up in weights:
        pre_gate = plain(x_rows, gate)
        pre_up = plain(x_rows, up)
        sigmoid = 1.0 / (1.0 + jnp.exp(-pre_gate))
        activated = pre_gate * sigmoid
        hidden.append((activated * pre_up).astype(BF16))
        active.append(activated)
        slope.append(pre_up * sigmoid * (1.0 + pre_gate * (1.0 - sigmoid)))
    return hidden, active, slope


def backward_values(s_rows, active, slope, weights):
    total = None
    for activated, steep, (gate, up, down) in zip(active, slope, weights):
        hidden_grad = contract_last(s_rows, down)
        gate_grad = (hidden_grad * steep).astype(BF16)
        up_grad = (hidden_grad * activated).astype(BF16)
        piece = contract_last(gate_grad, gate) + contract_last(up_grad, up)
        piece = piece.astype(BF16).astype(F32)
        total = piece if total is None else total + piece
    return total


def polynomial_core(scaled, hidden, width, own):
    exact = lax.Precision.HIGHEST
    rows = scaled.shape[0]
    left = contract_last(scaled, scaled)
    right = contract_last(hidden, hidden)
    squares = jnp.maximum(jnp.sum(left * right), 0.0)
    inverse = 1.0 / (jnp.sqrt(squares) + 1e-07)
    row = lax.broadcasted_iota(jnp.int32, (rows, rows), 0)
    col = lax.broadcasted_iota(jnp.int32, (rows, rows), 1)
    eye = jnp.where(row == col, linear_term, 0.0)
    moment = plain(left * inverse, right * inverse, exact)
    core = None
    for iteration in range(ITERS):
        factor = eye + cubic_term * moment + quintic_term * plain(moment, moment, exact)
        core = factor if core is None else plain(factor, core, exact)
        if iteration < ITERS - 1:
            moment = plain(plain(moment, factor, exact), factor, exact)
    core = core * (inverse * math.sqrt(width))
    mixed = dot(core, own.astype(F32), ((0,), (0,)), exact)
    high = mixed.astype(BF16).astype(F32)
    stacked = jnp.transpose(jnp.concatenate([high, mixed - high], axis=0)).astype(BF16)
    return plain(stacked, jnp.concatenate([scaled, scaled], axis=0)).astype(BF16)


def vmem(value):
    return pltpu.with_memory_space_constraint(value, pltpu.VMEM)


SPEC = pl.BlockSpec(memory_space=pltpu.VMEM)


def call(body, shapes, args, flops, limit=16 << 20):
    return pl.pallas_call(
        body,
        out_shape=shapes,
        in_specs=[SPEC] * len(args),
        out_specs=[SPEC] * len(shapes),
        compiler_params=pltpu.CompilerParams(vmem_limit_bytes=limit),
        cost_estimate=pl.CostEstimate(flops=flops, bytes_accessed=0, transcendentals=0),
    )(*args)


def kept(shape, dtype):
    return pltpu.VMEM(shape, dtype)


def pairs(refs):
    values = [r[...].astype(F32) for r in refs]
    half = values[0].shape[0] // 2
    x_rows = jnp.concatenate([v[:half] for v in values], axis=0).astype(BF16)
    s_rows = jnp.concatenate([v[half:] for v in values], axis=0).astype(BF16)
    return x_rows, s_rows


def swap_half(value):
    halves = lax.axis_size("half")
    return lax.ppermute(value, "half", [(i, (i + 1) % halves) for i in range(halves)])


def small_program(
    x, u, routes, gates, own, tokens_dev, experts, capacity, hidden_units
):
    rows, width = x.shape
    block = rows // tokens_dev * capacity
    slots = experts * block
    units = own[0].shape[1]

    def dispatch_body(x_ref, u_ref, routes_ref, gates_ref, *outs):
        base = lax.axis_index("expert")
        x_rows, s_rows, pick = route_rows(
            x_ref[...], u_ref[...], routes_ref[...], gates_ref[...],
            base, tokens_dev, experts, capacity,
        )
        for d in range(experts):
            at = d * block
            both = jnp.concatenate([x_rows[at : at + block], s_rows[at : at + block]], axis=0)
            outs[d][...] = both.astype(BF16)
        outs[experts][...] = pick

    *blocks, pick = call(
        dispatch_body,
        [kept((2 * block, width), BF16)] * experts + [kept((rows, slots), BF16)],
        [x, u, routes, gates],
        10**7,
    )

    def shift(value, by):
        return lax.ppermute(
            value, "expert", [(i, (i + by) % experts) for i in range(experts)]
        )

    got = [blocks[0]] + [shift(blocks[d], d) for d in range(1, experts)]
    other = [swap_half(w) for w in own]

    def forward_body(*refs):
        n = experts
        gate_own, up_own, gate_other, up_other = refs[n : n + 4]
        outs = refs[n + 4 :]
        x_rows, s_rows = pairs(refs[:n])
        weights = [(gate_own[...], up_own[...]), (gate_other[...], up_other[...])]
        hidden, active, slope = forward_values(x_rows, weights)
        outs[0][:, :units] = hidden[1]
        outs[0][:, units : 2 * units] = hidden[0]
        outs[0][:, 2 * units :] = s_rows
        outs[1][:, :units] = hidden[0]
        outs[1][:, units : 2 * units] = hidden[1]
        outs[1][:, 2 * units :] = s_rows
        outs[2][...] = jnp.concatenate(active, axis=1)
        outs[3][...] = jnp.concatenate(slope, axis=1)

    packed = 2 * units + width
    to_other, mine, active, slope = call(
        forward_body,
        [kept((slots, packed), BF16)] * 2 + [kept((slots, 2 * units), F32)] * 2,
        [vmem(g) for g in got] + [vmem(w) for w in (own[0], own[1], other[0], other[1])],
        2 * slots * width * units * 4,
    )
    theirs = swap_half(to_other)

    def backward_body(mine_ref, active_ref, slope_ref, *refs):
        weights = [tuple(r[...] for r in refs[:3]), tuple(r[...] for r in refs[3:6])]
        outs = refs[6:]
        cut = lambda r: [r[:, :units], r[:, units:]]
        total = backward_values(
            mine_ref[:, 2 * units :], cut(active_ref), cut(slope_ref), weights
        )
        for d in range(experts):
            outs[d][...] = total[d * block : (d + 1) * block].astype(BF16)

    grads = call(
        backward_body,
        [kept((block, width), BF16)] * experts,
        [vmem(v) for v in (mine, active, slope, *own, *other)],
        2 * slots * width * units * 6,
    )
    back = [grads[0]] + [shift(grads[d], experts - d) for d in range(1, experts)]

    def core_body(mine_ref, theirs_ref, out_ref):
        both = jnp.concatenate(
            [mine_ref[...].astype(F32), theirs_ref[...].astype(F32)], axis=0
        ).astype(BF16)
        out_ref[...] = polynomial_core(
            both[:, 2 * units :], both[:, : 2 * units], max(hidden_units, width), both[:, :units]
        )

    (update,) = call(
        core_body,
        [jax.ShapeDtypeStruct((units, width), BF16)],
        [vmem(mine), vmem(theirs)],
        2 * 4 * slots * width * units * 2,
    )

    def combine_body(pick_ref, *refs):
        rows_back = jnp.concatenate([r[...].astype(F32) for r in refs[:-1]], axis=0)
        refs[-1][...] = plain(pick_ref[...], rows_back.astype(BF16)).astype(BF16)

    (cotangent,) = call(
        combine_body,
        [jax.ShapeDtypeStruct((rows, width), BF16)],
        [vmem(pick)] + [vmem(b) for b in back],
        10**6,
    )
    return cotangent, update


def large_program(
    x, u, routes, gates, own, tokens_dev, experts, capacity, hidden_units
):
    rows, width = x.shape
    block = rows // tokens_dev * capacity
    slots = experts * block
    units = own[0].shape[1]
    x_rows, s_rows, pick = route_rows(
        x, u, routes, gates, 0, tokens_dev, experts, capacity
    )
    other = [swap_half(w) for w in own]
    sent = jnp.stack([x_rows.astype(BF16), s_rows.astype(BF16)])
    sent = sent.reshape(2, experts, block, width)
    got = lax.all_to_all(sent, "expert", split_axis=1, concat_axis=1, tiled=True)
    x_rows = got[0].reshape(slots, width)
    s_rows = got[1].reshape(slots, width)
    hidden, active, slope = forward_values(x_rows, [own[:2], other[:2]])
    theirs = swap_half(jnp.concatenate([hidden[1], hidden[0], s_rows], axis=1))
    mine = jnp.concatenate([hidden[0], hidden[1], s_rows], axis=1)
    total = backward_values(s_rows, active, slope, [own, other])
    total = total.astype(BF16).reshape(experts, block, width)
    back = lax.all_to_all(total, "expert", split_axis=0, concat_axis=0, tiled=True)
    cotangent = plain(pick, back.reshape(slots, width)).astype(BF16)
    both = jnp.concatenate([mine, theirs], axis=0)
    update = polynomial_core(
        both[:, 2 * units :], both[:, : 2 * units], max(hidden_units, width), both[:, :units]
    )
    return cotangent, update


def on_device(activations, upstream, routes, route_gates, gate_matrix, up_matrix, down_matrix):
    experts = lax.axis_size("expert")
    halves = lax.axis_size("half")
    batches, tokens_dev, top = routes.shape
    width = activations.shape[2]
    capacity = max(2, 6 * tokens_dev * top // (5 * experts))
    rows = batches * tokens_dev
    own = (gate_matrix[0], up_matrix[0], down_matrix[0])
    hidden_units = down_matrix.shape[1] * halves
    program = small_program if experts <= MAX_PERMUTED else large_program
    cotangent, update = program(
        activations.reshape(rows, width),
        upstream.reshape(rows, width),
        routes.reshape(rows, top),
        route_gates.reshape(rows, top),
        own, tokens_dev, experts, capacity, hidden_units,
    )
    return cotangent.reshape(batches, tokens_dev, width), update[None]


def solution(mesh):
    tokens = P(None, ("dp", "expert", "half"), None)
    return jax.shard_map(
        on_device,
        mesh=mesh,
        in_specs=(tokens,) * 4
        + (P("expert", None, "half"), P("expert", None, "half"), P("expert", "half", None)),
        out_specs=(tokens, P(("dp", "expert"), "half", None)),
        check_vma=False,
    )
```

```python
import functools
import math

import jax
import jax.numpy as jnp
from jax import lax
from jax.experimental import pallas as pl
from jax.experimental.pallas import tpu as pltpu
from jax.sharding import PartitionSpec as P

ITERS = 2
MAX_PERMUTED = 8

linear_term = 3.4445
cubic_term = -4.775
quintic_term = 2.0315

F32 = jnp.float32
BF16 = jnp.bfloat16


def dot(left, right, dims, precision=None):
    return lax.dot_general(
        left, right, (dims, ((), ())), precision=precision, preferred_element_type=F32
    )


def contract_last(left, right):
    return dot(left, right, ((1,), (1,)))


def plain(left, right, precision=None):
    return dot(left, right, ((1,), (0,)), precision)


def route_slots(routes, base, experts, block, capacity):
    tokens_dev = routes[0].shape[1]
    expert_ids = lax.broadcasted_iota(jnp.int32, (experts, tokens_dev), 0)
    row = lax.broadcasted_iota(jnp.int32, (tokens_dev, tokens_dev), 0)
    col = lax.broadcasted_iota(jnp.int32, (tokens_dev, tokens_dev), 1)
    earlier = jnp.where(row < col, 1.0, 0.0).astype(BF16)
    found = []
    for batch, named in enumerate(routes):
        top = named.shape[0]
        onehots = [jnp.where(named[k : k + 1] == expert_ids, 1.0, 0.0) for k in range(top)]
        before = plain(sum(onehots).astype(BF16), earlier)
        slots = []
        for k in range(top):
            position = jnp.sum(before * onehots[k], axis=0, keepdims=True).astype(jnp.int32)
            before = before + onehots[k]
            relative = named[k : k + 1] - base
            relative = jnp.where(relative < 0, relative + experts, relative)
            slots.append((relative, batch * capacity + position))
        found.append(slots)
    return found


def route_rows(data, routes, gates, base, experts, capacity):
    batches, top = len(routes), routes[0].shape[0]
    block = batches * capacity
    found = route_slots(routes, base, experts, block, capacity)
    joined = lambda rows: jnp.concatenate(rows, axis=1)
    tokens = data.shape[0] // 2
    row = lax.broadcasted_iota(jnp.int32, (2 * experts * block, tokens), 0)
    slot = lax.broadcasted_iota(jnp.int32, (experts * block, tokens), 0)
    in_x = row[:, :1] % (2 * block) < block
    pick_x, pick_u, pick_tok, gate = 0.0, 0.0, 0.0, jnp.where(in_x, 1.0, 0.0)
    for k in range(top):
        relative = joined([found[m][k][0] for m in range(batches)])
        within = joined([found[m][k][1] for m in range(batches)])
        gates_k = joined([gates[m][k : k + 1] for m in range(batches)])
        at = relative * (2 * block) + within
        here = row == at + block
        pick_x = pick_x + jnp.where(row == at, 1.0, 0.0)
        pick_u = pick_u + jnp.where(here, 1.0, 0.0)
        pick_tok = pick_tok + jnp.where(slot == relative * block + within, 1.0, 0.0)
        gate = gate + jnp.sum(jnp.where(here, gates_k, 0.0), axis=1, keepdims=True)
    picks = joined([pick_x, pick_u]).astype(BF16)
    return plain(picks, data) * gate, pick_tok


def forward_values(x_rows, weights):
    hidden, active, slope = [], [], []
    for gate, up in weights:
        pre_gate = plain(x_rows, gate)
        pre_up = plain(x_rows, up)
        sigmoid = 1.0 / (1.0 + jnp.exp(-pre_gate))
        activated = pre_gate * sigmoid
        hidden.append((activated * pre_up).astype(BF16))
        active.append(activated)
        slope.append(pre_up * sigmoid * (1.0 + pre_gate * (1.0 - sigmoid)))
    return hidden, active, slope


def backward_values(s_rows, active, slope, weights):
    total = None
    for activated, steep, (gate, up, down) in zip(active, slope, weights):
        hidden_grad = contract_last(s_rows, down)
        gate_grad = (hidden_grad * steep).astype(BF16)
        up_grad = (hidden_grad * activated).astype(BF16)
        piece = contract_last(gate_grad, gate) + contract_last(up_grad, up)
        piece = piece.astype(BF16).astype(F32)
        total = piece if total is None else total + piece
    return total


def polynomial_core(scaled, hidden, width, own):
    exact = lax.Precision.HIGHEST
    rows = scaled.shape[0]
    left = contract_last(scaled, scaled)
    right = contract_last(hidden, hidden)
    squares = jnp.maximum(jnp.sum(left * right), 0.0)
    inverse = 1.0 / (jnp.sqrt(squares) + 1e-07)
    row = lax.broadcasted_iota(jnp.int32, (rows, rows), 0)
    col = lax.broadcasted_iota(jnp.int32, (rows, rows), 1)
    eye = jnp.where(row == col, linear_term, 0.0)
    moment = plain(left * inverse, right * inverse, exact)
    core = None
    for iteration in range(ITERS):
        factor = eye + cubic_term * moment + quintic_term * plain(moment, moment, exact)
        core = factor if core is None else plain(factor, core, exact)
        if iteration < ITERS - 1:
            moment = plain(plain(moment, factor, exact), factor, exact)
    core = core * (inverse * math.sqrt(width))
    mixed = dot(core, own.astype(F32), ((0,), (0,)), exact)
    high = mixed.astype(BF16).astype(F32)
    stacked = jnp.transpose(jnp.concatenate([high, mixed - high], axis=0)).astype(BF16)
    return plain(stacked, jnp.concatenate([scaled, scaled], axis=0)).astype(BF16)


def vmem(value):
    return pltpu.with_memory_space_constraint(value, pltpu.VMEM)


def hbm(value):
    return pltpu.with_memory_space_constraint(value, pltpu.HBM)


IN_VMEM = pl.BlockSpec(memory_space=pltpu.VMEM)
IN_HBM = pl.BlockSpec(memory_space=pltpu.HBM)


def call(body, shapes, args, flops, specs=None, scratch=(), limit=16 << 20):
    return pl.pallas_call(
        body,
        out_shape=shapes,
        in_specs=specs or [IN_VMEM] * len(args),
        out_specs=[IN_VMEM] * len(shapes),
        scratch_shapes=scratch,
        compiler_params=pltpu.CompilerParams(vmem_limit_bytes=limit),
        cost_estimate=pl.CostEstimate(flops=flops, bytes_accessed=0, transcendentals=0),
    )(*args)


def kept(shape, dtype):
    return pltpu.VMEM(shape, dtype)


def pairs(refs):
    values = [r[...].astype(F32) for r in refs]
    half = values[0].shape[0] // 2
    x_rows = jnp.concatenate([v[:half] for v in values], axis=0).astype(BF16)
    s_rows = jnp.concatenate([v[half:] for v in values], axis=0).astype(BF16)
    return x_rows, s_rows


def swap_half(value):
    halves = lax.axis_size("half")
    return lax.ppermute(value, "half", [(i, (i + 1) % halves) for i in range(halves)])


def small_program(activations, upstream, routes, gates, own, experts, capacity, hidden_units):
    batches, top, tokens_dev = routes.shape
    width = activations.shape[1]
    rows = batches * tokens_dev
    block = batches * capacity
    slots = experts * block
    units = own[0].shape[1]

    def dispatch_body(x_hbm, u_hbm, routes_hbm, gates_hbm, *refs):
        *outs, pick_ref, data, routes_ref, gates_ref, sems = refs
        copies = [
            pltpu.make_async_copy(routes_hbm, routes_ref, sems.at[0]),
            pltpu.make_async_copy(gates_hbm, gates_ref, sems.at[1]),
            pltpu.make_async_copy(x_hbm, data.at[:rows], sems.at[2]),
            pltpu.make_async_copy(u_hbm, data.at[rows:], sems.at[3]),
        ]
        for copy in copies:
            copy.start()
        for copy in copies:
            copy.wait()
        sent, pick = route_rows(
            data[...],
            [routes_ref[m] for m in range(batches)],
            [gates_ref[m] for m in range(batches)],
            lax.axis_index("expert"), experts, capacity,
        )
        for d in range(experts):
            outs[d][...] = sent[2 * d * block : 2 * (d + 1) * block].astype(BF16)
        pick_ref[...] = pick

    *blocks, pick = call(
        dispatch_body,
        [kept((2 * block, width), BF16)] * experts + [kept((slots, rows), F32)],
        [hbm(v) for v in (activations, upstream, routes, gates)],
        10**7,
        specs=[IN_HBM] * 4,
        scratch=[
            pltpu.VMEM((2 * rows, width), BF16),
            pltpu.VMEM((batches, top, tokens_dev), jnp.int32),
            pltpu.VMEM((batches, top, tokens_dev), F32),
            pltpu.SemaphoreType.DMA((4,)),
        ],
    )

    def shift(value, by):
        return lax.ppermute(
            value, "expert", [(i, (i + by) % experts) for i in range(experts)]
        )

    held, blocks = lax.optimization_barrier((own, blocks))
    got = [blocks[0]] + [shift(blocks[d], d) for d in range(1, experts)]
    other = [swap_half(w) for w in held]

    def fetch_body(pick_ref, *refs):
        ins, outs, sems = refs[:3], refs[3:6], refs[7]
        copies = [pltpu.make_async_copy(ins[i], outs[i], sems.at[i]) for i in range(3)]
        for copy in copies:
            copy.start()
        refs[6][...] = jnp.transpose(pick_ref[...]).astype(BF16)
        for copy in copies:
            copy.wait()

    *near, pick = call(
        fetch_body,
        [kept(w.shape, BF16) for w in own] + [kept((rows, slots), BF16)],
        [vmem(pick)] + [hbm(w) for w in held],
        10**9,
        specs=[IN_VMEM] + [IN_HBM] * 3,
        scratch=[pltpu.SemaphoreType.DMA((3,))],
    )

    def expert_body(*refs):
        weights = [tuple(r[...] for r in refs[experts + 3 * i :][:3]) for i in range(2)]
        to_other, mine, *outs = refs[experts + 6 :]
        x_rows, s_rows = pairs(refs[:experts])
        hidden, active, slope = forward_values(x_rows, [w[:2] for w in weights])
        to_other[:, :units] = hidden[1]
        to_other[:, units : 2 * units] = hidden[0]
        to_other[:, 2 * units :] = s_rows
        mine[:, :units] = hidden[0]
        mine[:, units : 2 * units] = hidden[1]
        mine[:, 2 * units :] = s_rows
        total = backward_values(s_rows, active, slope, weights)
        for d in range(experts):
            outs[d][...] = total[d * block : (d + 1) * block].astype(BF16)

    to_other, mine, *grads = call(
        expert_body,
        [kept((slots, 2 * units + width), BF16)] * 2 + [kept((block, width), BF16)] * experts,
        [vmem(v) for v in (*got, *near, *other)],
        2 * slots * width * units * 10,
    )
    back = [grads[0]] + [shift(grads[d], experts - d) for d in range(1, experts)]
    theirs = swap_half(to_other)

    def core_body(mine_ref, theirs_ref, out_ref):
        both = jnp.concatenate(
            [mine_ref[...].astype(F32), theirs_ref[...].astype(F32)], axis=0
        ).astype(BF16)
        out_ref[...] = polynomial_core(
            both[:, 2 * units :], both[:, : 2 * units], max(hidden_units, width), both[:, :units]
        )

    (update,) = call(
        core_body,
        [jax.ShapeDtypeStruct((units, width), BF16)],
        [vmem(mine), vmem(theirs)],
        2 * 4 * slots * width * units * 2,
    )
    update, back = lax.optimization_barrier((update, back))

    def combine_body(pick_ref, *refs):
        rows_back = jnp.concatenate([r[...].astype(F32) for r in refs[:-1]], axis=0)
        refs[-1][...] = plain(pick_ref[...], rows_back.astype(BF16)).astype(BF16)

    (cotangent,) = call(
        combine_body,
        [jax.ShapeDtypeStruct((rows, width), BF16)],
        [vmem(pick)] + [vmem(b) for b in back],
        10**6,
    )
    return cotangent, update


def large_program(activations, upstream, routes, gates, own, experts, capacity, hidden_units):
    batches, top, tokens_dev = routes.shape
    width = activations.shape[1]
    block = batches * capacity
    slots = experts * block
    units = own[0].shape[1]
    sent, pick = route_rows(
        jnp.concatenate([activations, upstream], axis=0), routes, gates, 0, experts, capacity
    )
    other = [swap_half(w) for w in own]
    sent = sent.astype(BF16).reshape(experts, 2 * block, width)
    got = lax.all_to_all(sent, "expert", split_axis=0, concat_axis=0, tiled=True)
    x_rows = got[:, :block].reshape(slots, width)
    s_rows = got[:, block:].reshape(slots, width)
    hidden, active, slope = forward_values(x_rows, [own[:2], other[:2]])
    theirs = swap_half(jnp.concatenate([hidden[1], hidden[0], s_rows], axis=1))
    mine = jnp.concatenate([hidden[0], hidden[1], s_rows], axis=1)
    total = backward_values(s_rows, active, slope, [own, other])
    total = total.astype(BF16).reshape(experts, block, width)
    back = lax.all_to_all(total, "expert", split_axis=0, concat_axis=0, tiled=True)
    cotangent = dot(pick.astype(BF16), back.reshape(slots, width), ((0,), (0,))).astype(BF16)
    both = jnp.concatenate([mine, theirs], axis=0)
    update = polynomial_core(
        both[:, 2 * units :], both[:, : 2 * units], max(hidden_units, width), both[:, :units]
    )
    return cotangent, update


def on_device(activations, upstream, routes, route_gates, gate_matrix, up_matrix, down_matrix):
    experts = lax.axis_size("expert")
    halves = lax.axis_size("half")
    batches, tokens_dev, top = routes.shape
    width = activations.shape[2]
    capacity = max(2, 6 * tokens_dev * top // (5 * experts))
    rows = batches * tokens_dev
    own = (gate_matrix[0], up_matrix[0], down_matrix[0])
    hidden_units = down_matrix.shape[1] * halves
    program = small_program if experts <= MAX_PERMUTED else large_program
    cotangent, update = program(
        activations.reshape(rows, width),
        upstream.reshape(rows, width),
        jnp.swapaxes(routes, 1, 2),
        jnp.swapaxes(route_gates, 1, 2),
        own, experts, capacity, hidden_units,
    )
    return cotangent.reshape(batches, tokens_dev, width), update[None]


def solution(mesh):
    tokens = P(None, ("dp", "expert", "half"), None)
    return jax.shard_map(
        on_device,
        mesh=mesh,
        in_specs=(tokens,) * 4
        + (P("expert", None, "half"), P("expert", None, "half"), P("expert", "half", None)),
        out_specs=(tokens, P(("dp", "expert"), "half", None)),
        check_vma=False,
    )
```

```python
import functools
import math

import jax
import jax.numpy as jnp
from jax import lax
from jax.experimental import pallas as pl
from jax.experimental.pallas import tpu as pltpu
from jax.sharding import PartitionSpec as P

ITERS = 2
MAX_PERMUTED = 8

linear_term = 3.4445
cubic_term = -4.775
quintic_term = 2.0315

F32 = jnp.float32
BF16 = jnp.bfloat16


def dot(left, right, dims, precision=None):
    return lax.dot_general(
        left, right, (dims, ((), ())), precision=precision, preferred_element_type=F32
    )


def contract_last(left, right):
    return dot(left, right, ((1,), (1,)))


def plain(left, right, precision=None):
    return dot(left, right, ((1,), (0,)), precision)


def route_slots(routes, base, experts, block, capacity):
    tokens_dev = routes[0].shape[1]
    expert_ids = lax.broadcasted_iota(jnp.int32, (experts, tokens_dev), 0)
    row = lax.broadcasted_iota(jnp.int32, (tokens_dev, tokens_dev), 0)
    col = lax.broadcasted_iota(jnp.int32, (tokens_dev, tokens_dev), 1)
    earlier = jnp.where(row < col, 1.0, 0.0).astype(BF16)
    found = []
    for batch, named in enumerate(routes):
        top = named.shape[0]
        onehots = [jnp.where(named[k : k + 1] == expert_ids, 1.0, 0.0) for k in range(top)]
        before = plain(sum(onehots).astype(BF16), earlier)
        slots = []
        for k in range(top):
            position = jnp.sum(before * onehots[k], axis=0, keepdims=True).astype(jnp.int32)
            before = before + onehots[k]
            relative = named[k : k + 1] - base
            relative = jnp.where(relative < 0, relative + experts, relative)
            slots.append((relative, batch * capacity + position))
        found.append(slots)
    return found


def route_rows(data, routes, gates, base, experts, capacity):
    batches, top = len(routes), routes[0].shape[0]
    block = batches * capacity
    found = route_slots(routes, base, experts, block, capacity)
    joined = lambda rows: jnp.concatenate(rows, axis=1)
    tokens = data.shape[0] // 2
    row = lax.broadcasted_iota(jnp.int32, (2 * experts * block, tokens), 0)
    slot = lax.broadcasted_iota(jnp.int32, (experts * block, tokens), 0)
    in_x = row[:, :1] % (2 * block) < block
    pick_x, pick_u, pick_tok, gate = 0.0, 0.0, 0.0, jnp.where(in_x, 1.0, 0.0)
    for k in range(top):
        relative = joined([found[m][k][0] for m in range(batches)])
        within = joined([found[m][k][1] for m in range(batches)])
        gates_k = joined([gates[m][k : k + 1] for m in range(batches)])
        at = relative * (2 * block) + within
        here = row == at + block
        pick_x = pick_x + jnp.where(row == at, 1.0, 0.0)
        pick_u = pick_u + jnp.where(here, 1.0, 0.0)
        pick_tok = pick_tok + jnp.where(slot == relative * block + within, 1.0, 0.0)
        gate = gate + jnp.sum(jnp.where(here, gates_k, 0.0), axis=1, keepdims=True)
    picks = joined([pick_x, pick_u]).astype(BF16)
    return plain(picks, data) * gate, pick_tok


def forward_values(x_rows, weights):
    hidden, active, slope = [], [], []
    for gate, up, _ in weights:
        pre_gate = plain(x_rows, gate)
        pre_up = plain(x_rows, up)
        sigmoid = 1.0 / (1.0 + jnp.exp(-pre_gate))
        activated = pre_gate * sigmoid
        hidden.append((activated * pre_up).astype(BF16))
        active.append(activated)
        slope.append(pre_up * sigmoid * (1.0 + pre_gate * (1.0 - sigmoid)))
    return hidden, active, slope


def backward_values(s_rows, active, slope, weights):
    total = None
    for activated, steep, (gate, up, down) in zip(active, slope, weights):
        wide = s_rows.shape[1] // len(down)
        hidden_grad = sum(
            contract_last(s_rows[:, c * wide : (c + 1) * wide], block)
            for c, block in enumerate(down)
        )
        gate_grad = (hidden_grad * steep).astype(BF16)
        up_grad = (hidden_grad * activated).astype(BF16)
        piece = contract_last(gate_grad, gate) + contract_last(up_grad, up)
        piece = piece.astype(BF16).astype(F32)
        total = piece if total is None else total + piece
    return total


def polynomial_core(scaled, hidden, width, own):
    exact = lax.Precision.HIGHEST
    rows = scaled.shape[0]
    left = contract_last(scaled, scaled)
    right = contract_last(hidden, hidden)
    squares = jnp.maximum(jnp.sum(left * right), 0.0)
    inverse = 1.0 / (jnp.sqrt(squares) + 1e-07)
    row = lax.broadcasted_iota(jnp.int32, (rows, rows), 0)
    col = lax.broadcasted_iota(jnp.int32, (rows, rows), 1)
    eye = jnp.where(row == col, linear_term, 0.0)
    moment = plain(left * inverse, right * inverse, exact)
    core = None
    for iteration in range(ITERS):
        factor = eye + cubic_term * moment + quintic_term * plain(moment, moment, exact)
        core = factor if core is None else plain(factor, core, exact)
        if iteration < ITERS - 1:
            moment = plain(plain(moment, factor, exact), factor, exact)
    core = core * (inverse * math.sqrt(width))
    mixed = dot(core, own.astype(F32), ((0,), (0,)), exact)
    high = mixed.astype(BF16).astype(F32)
    stacked = jnp.transpose(jnp.concatenate([high, mixed - high], axis=0)).astype(BF16)
    return plain(stacked, jnp.concatenate([scaled, scaled], axis=0)).astype(BF16)


def vmem(value):
    return pltpu.with_memory_space_constraint(value, pltpu.VMEM)


def hbm(value):
    return pltpu.with_memory_space_constraint(value, pltpu.HBM)


IN_VMEM = pl.BlockSpec(memory_space=pltpu.VMEM)
IN_HBM = pl.BlockSpec(memory_space=pltpu.HBM)


def call(body, shapes, args, flops, specs=None, scratch=(), limit=16 << 20):
    return pl.pallas_call(
        body,
        out_shape=shapes,
        in_specs=specs or [IN_VMEM] * len(args),
        out_specs=[IN_VMEM] * len(shapes),
        scratch_shapes=scratch,
        compiler_params=pltpu.CompilerParams(vmem_limit_bytes=limit),
        cost_estimate=pl.CostEstimate(flops=flops, bytes_accessed=0, transcendentals=0),
    )(*args)


def kept(shape, dtype):
    return pltpu.VMEM(shape, dtype)


def pairs(refs):
    values = [r[...].astype(F32) for r in refs]
    half = values[0].shape[0] // 2
    x_rows = jnp.concatenate([v[:half] for v in values], axis=0).astype(BF16)
    s_rows = jnp.concatenate([v[half:] for v in values], axis=0).astype(BF16)
    return x_rows, s_rows


def swap_half(value):
    halves = lax.axis_size("half")
    return lax.ppermute(value, "half", [(i, (i + 1) % halves) for i in range(halves)])


def small_program(activations, upstream, routes, gates, own, experts, capacity, hidden_units):
    batches, top, tokens_dev = routes.shape
    width = activations.shape[1]
    rows = batches * tokens_dev
    block = batches * capacity
    slots = experts * block
    units = own[0].shape[1]

    far = [swap_half(w) for w in own]

    def dispatch_body(x_hbm, u_hbm, routes_hbm, gates_hbm, *refs):
        *outs, pick_ref, data, routes_ref, gates_ref, sems = refs
        copies = [
            pltpu.make_async_copy(routes_hbm, routes_ref, sems.at[0]),
            pltpu.make_async_copy(gates_hbm, gates_ref, sems.at[1]),
            pltpu.make_async_copy(x_hbm, data.at[:rows], sems.at[2]),
            pltpu.make_async_copy(u_hbm, data.at[rows:], sems.at[3]),
        ]
        for copy in copies:
            copy.start()
        for copy in copies:
            copy.wait()
        sent, pick = route_rows(
            data[...],
            [routes_ref[m] for m in range(batches)],
            [gates_ref[m] for m in range(batches)],
            lax.axis_index("expert"), experts, capacity,
        )
        for d in range(experts):
            outs[d][...] = sent[2 * d * block : 2 * (d + 1) * block].astype(BF16)
        pick_ref[...] = pick

    *blocks, pick = call(
        dispatch_body,
        [kept((2 * block, width), BF16)] * experts + [kept((slots, rows), F32)],
        [hbm(v) for v in (activations, upstream, routes, gates)],
        10**7,
        specs=[IN_HBM] * 4,
        scratch=[
            pltpu.VMEM((2 * rows, width), BF16),
            pltpu.VMEM((batches, top, tokens_dev), jnp.int32),
            pltpu.VMEM((batches, top, tokens_dev), F32),
            pltpu.SemaphoreType.DMA((4,)),
        ],
    )

    def shift(value, by):
        return lax.ppermute(
            value, "expert", [(i, (i + by) % experts) for i in range(experts)]
        )

    blocks[-1], far[0] = lax.optimization_barrier((blocks[-1], far[0]))
    got = [blocks[0]] + [shift(blocks[d], d) for d in range(1, experts)]

    def fetch_body(pick_ref, *refs):
        ins, outs, sems = refs[:3], refs[3:6], refs[7]
        copies = [pltpu.make_async_copy(ins[i], outs[i], sems.at[i]) for i in range(3)]
        for copy in copies:
            copy.start()
        refs[6][...] = jnp.transpose(pick_ref[...]).astype(BF16)
        for copy in copies:
            copy.wait()

    *near, pick = call(
        fetch_body,
        [kept(w.shape, BF16) for w in own] + [kept((rows, slots), BF16)],
        [vmem(pick)] + [hbm(w) for w in own],
        10**9,
        specs=[IN_VMEM] + [IN_HBM] * 3,
        scratch=[pltpu.SemaphoreType.DMA((3,))],
    )

    def expert_body(*refs):
        held = [r[...] for r in refs[experts : experts + 6]]
        weights = [(*held[:2], [held[2]]), (*held[3:5], [held[5]])]
        to_other, mine, *outs = refs[experts + 6 :]
        x_rows, s_rows = pairs(refs[:experts])
        hidden, active, slope = forward_values(x_rows, weights)
        to_other[:, :units] = hidden[1]
        to_other[:, units : 2 * units] = hidden[0]
        to_other[:, 2 * units :] = s_rows
        mine[:, :units] = hidden[0]
        mine[:, units : 2 * units] = hidden[1]
        mine[:, 2 * units :] = s_rows
        total = backward_values(s_rows, active, slope, weights)
        for d in range(experts):
            outs[d][...] = total[d * block : (d + 1) * block].astype(BF16)

    to_other, mine, *grads = call(
        expert_body,
        [kept((slots, 2 * units + width), BF16)] * 2 + [kept((block, width), BF16)] * experts,
        [vmem(v) for v in (*got, *near, *far)],
        2 * slots * width * units * 10,
    )
    back = [grads[0]] + [shift(grads[d], experts - d) for d in range(1, experts)]
    theirs = swap_half(to_other)

    def core_body(mine_ref, theirs_ref, out_ref):
        both = jnp.concatenate(
            [mine_ref[...].astype(F32), theirs_ref[...].astype(F32)], axis=0
        ).astype(BF16)
        out_ref[...] = polynomial_core(
            both[:, 2 * units :], both[:, : 2 * units], max(hidden_units, width), both[:, :units]
        )

    (update,) = call(
        core_body,
        [jax.ShapeDtypeStruct((units, width), BF16)],
        [vmem(mine), vmem(theirs)],
        2 * 4 * slots * width * units * 2,
    )
    update, back = lax.optimization_barrier((update, back))

    def combine_body(pick_ref, *refs):
        rows_back = jnp.concatenate([r[...].astype(F32) for r in refs[:-1]], axis=0)
        refs[-1][...] = plain(pick_ref[...], rows_back.astype(BF16)).astype(BF16)

    (cotangent,) = call(
        combine_body,
        [jax.ShapeDtypeStruct((rows, width), BF16)],
        [vmem(pick)] + [vmem(b) for b in back],
        10**6,
    )
    return cotangent, update


def large_program(activations, upstream, routes, gates, own, experts, capacity, hidden_units):
    batches, top, tokens_dev = routes.shape
    width = activations.shape[1]
    block = batches * capacity
    slots = experts * block
    units = own[0].shape[1]
    sent, pick = route_rows(
        jnp.concatenate([activations, upstream], axis=0), routes, gates, 0, experts, capacity
    )
    weights = [(*w[:2], [w[2]]) for w in (own, [swap_half(w) for w in own])]
    sent = sent.astype(BF16).reshape(experts, 2 * block, width)
    got = lax.all_to_all(sent, "expert", split_axis=0, concat_axis=0, tiled=True)
    x_rows = got[:, :block].reshape(slots, width)
    s_rows = got[:, block:].reshape(slots, width)
    hidden, active, slope = forward_values(x_rows, weights)
    theirs = swap_half(jnp.concatenate([hidden[1], hidden[0], s_rows], axis=1))
    mine = jnp.concatenate([hidden[0], hidden[1], s_rows], axis=1)
    total = backward_values(s_rows, active, slope, weights)
    total = total.astype(BF16).reshape(experts, block, width)
    back = lax.all_to_all(total, "expert", split_axis=0, concat_axis=0, tiled=True)
    cotangent = dot(pick.astype(BF16), back.reshape(slots, width), ((0,), (0,))).astype(BF16)
    both = jnp.concatenate([mine, theirs], axis=0)
    update = polynomial_core(
        both[:, 2 * units :], both[:, : 2 * units], max(hidden_units, width), both[:, :units]
    )
    return cotangent, update


def on_device(activations, upstream, routes, route_gates, gate_matrix, up_matrix, down_matrix):
    experts = lax.axis_size("expert")
    halves = lax.axis_size("half")
    batches, tokens_dev, top = routes.shape
    width = activations.shape[2]
    capacity = max(2, 6 * tokens_dev * top // (5 * experts))
    rows = batches * tokens_dev
    own = (gate_matrix[0], up_matrix[0], down_matrix[0])
    hidden_units = down_matrix.shape[1] * halves
    program = small_program if experts <= MAX_PERMUTED else large_program
    cotangent, update = program(
        activations.reshape(rows, width),
        upstream.reshape(rows, width),
        jnp.swapaxes(routes, 1, 2),
        jnp.swapaxes(route_gates, 1, 2),
        own, experts, capacity, hidden_units,
    )
    return cotangent.reshape(batches, tokens_dev, width), update[None]


def solution(mesh):
    tokens = P(None, ("dp", "expert", "half"), None)
    return jax.shard_map(
        on_device,
        mesh=mesh,
        in_specs=(tokens,) * 4
        + (P("expert", None, "half"), P("expert", None, "half"), P("expert", "half", None)),
        out_specs=(tokens, P(("dp", "expert"), "half", None)),
        check_vma=False,
    )
```

```python
import functools
import math

import jax
import jax.numpy as jnp
from jax import lax
from jax.experimental import pallas as pl
from jax.experimental.pallas import tpu as pltpu
from jax.sharding import PartitionSpec as P

ITERS = 2
MAX_PERMUTED = 8
CHUNKS = 4

linear_term = 3.4445
cubic_term = -4.775
quintic_term = 2.0315

F32 = jnp.float32
BF16 = jnp.bfloat16


def dot(left, right, dims, precision=None):
    return lax.dot_general(
        left, right, (dims, ((), ())), precision=precision, preferred_element_type=F32
    )


def contract_last(left, right):
    return dot(left, right, ((1,), (1,)))


def plain(left, right, precision=None):
    return dot(left, right, ((1,), (0,)), precision)


def route_slots(routes, base, experts, block, capacity):
    tokens_dev = routes[0].shape[1]
    expert_ids = lax.broadcasted_iota(jnp.int32, (experts, tokens_dev), 0)
    row = lax.broadcasted_iota(jnp.int32, (tokens_dev, tokens_dev), 0)
    col = lax.broadcasted_iota(jnp.int32, (tokens_dev, tokens_dev), 1)
    earlier = jnp.where(row < col, 1.0, 0.0).astype(BF16)
    found = []
    for batch, named in enumerate(routes):
        top = named.shape[0]
        onehots = [jnp.where(named[k : k + 1] == expert_ids, 1.0, 0.0) for k in range(top)]
        before = plain(sum(onehots).astype(BF16), earlier)
        slots = []
        for k in range(top):
            position = jnp.sum(before * onehots[k], axis=0, keepdims=True).astype(jnp.int32)
            before = before + onehots[k]
            relative = named[k : k + 1] - base
            relative = jnp.where(relative < 0, relative + experts, relative)
            slots.append((relative, batch * capacity + position))
        found.append(slots)
    return found


def route_rows(data, routes, gates, base, experts, capacity):
    batches, top = len(routes), routes[0].shape[0]
    block = batches * capacity
    found = route_slots(routes, base, experts, block, capacity)
    joined = lambda rows: jnp.concatenate(rows, axis=1)
    tokens = data.shape[0] // 2
    row = lax.broadcasted_iota(jnp.int32, (2 * experts * block, tokens), 0)
    slot = lax.broadcasted_iota(jnp.int32, (experts * block, tokens), 0)
    in_x = row[:, :1] % (2 * block) < block
    pick_x, pick_u, pick_tok, gate = 0.0, 0.0, 0.0, jnp.where(in_x, 1.0, 0.0)
    for k in range(top):
        relative = joined([found[m][k][0] for m in range(batches)])
        within = joined([found[m][k][1] for m in range(batches)])
        gates_k = joined([gates[m][k : k + 1] for m in range(batches)])
        at = relative * (2 * block) + within
        here = row == at + block
        pick_x = pick_x + jnp.where(row == at, 1.0, 0.0)
        pick_u = pick_u + jnp.where(here, 1.0, 0.0)
        pick_tok = pick_tok + jnp.where(slot == relative * block + within, 1.0, 0.0)
        gate = gate + jnp.sum(jnp.where(here, gates_k, 0.0), axis=1, keepdims=True)
    picks = joined([pick_x, pick_u]).astype(BF16)
    return plain(picks, data) * gate, pick_tok


def forward_values(x_rows, weights):
    hidden, active, slope = [], [], []
    for gate, up, *_ in weights:
        pre_gate = plain(x_rows, gate)
        pre_up = plain(x_rows, up)
        sigmoid = 1.0 / (1.0 + jnp.exp(-pre_gate))
        activated = pre_gate * sigmoid
        hidden.append((activated * pre_up).astype(BF16))
        active.append(activated)
        slope.append(pre_up * sigmoid * (1.0 + pre_gate * (1.0 - sigmoid)))
    return hidden, active, slope


def backward_values(s_rows, active, slope, weights):
    total = None
    for activated, steep, (_, _, gate_turned, up_turned, down_turned) in zip(
        active, slope, weights
    ):
        hidden_grad = plain(s_rows, down_turned)
        gate_grad = (hidden_grad * steep).astype(BF16)
        up_grad = (hidden_grad * activated).astype(BF16)
        piece = plain(gate_grad, gate_turned) + plain(up_grad, up_turned)
        piece = piece.astype(BF16).astype(F32)
        total = piece if total is None else total + piece
    return total


def parts_of(value, count):
    parts = []
    for _ in range(count):
        part = value.astype(BF16)
        parts.append(part)
        value = value - part.astype(F32)
    return parts


def product(left, right, count):
    terms = [
        plain(l, r)
        for i, l in enumerate(left)
        for j, r in enumerate(right)
        if i + j < count
    ]
    return sum(terms[1:], terms[0])


def polynomial_core(scaled, hidden, units, width):
    rows = scaled.shape[0]
    own = jnp.transpose(hidden[:, :units].astype(F32)).astype(BF16)
    left = contract_last(scaled, scaled)
    right = contract_last(hidden, hidden)
    squares = jnp.maximum(jnp.sum(left * right), 0.0)
    inverse = 1.0 / (jnp.sqrt(squares) + 1e-07)
    row = lax.broadcasted_iota(jnp.int32, (rows, rows), 0)
    col = lax.broadcasted_iota(jnp.int32, (rows, rows), 1)
    eye = jnp.where(row == col, linear_term, 0.0)
    moment = product(parts_of(left * inverse, 3), parts_of(right * inverse, 3), 3)
    mixed = [own]
    for iteration in range(ITERS):
        halves = parts_of(moment, 2)
        if iteration == ITERS - 1:
            once = product(mixed, halves, 2)
            twice = product(parts_of(once, 2), halves, 2)
            mixed = linear_term * sum(m.astype(F32) for m in mixed)
            mixed = mixed + cubic_term * once + quintic_term * twice
        else:
            factor = eye + cubic_term * moment + quintic_term * product(halves, halves, 2)
            factor = parts_of(factor, 2)
            mixed = parts_of(product(mixed, factor, 2), 2)
            moment = product(parts_of(product(halves, factor, 2), 2), factor, 2)
    high, low = parts_of(mixed * (inverse * math.sqrt(width)), 2)
    both = jnp.concatenate([high.astype(F32), low.astype(F32)], axis=1).astype(BF16)
    return both, jnp.concatenate([scaled, scaled], axis=0)


def vmem(value):
    return pltpu.with_memory_space_constraint(value, pltpu.VMEM)


def hbm(value):
    return pltpu.with_memory_space_constraint(value, pltpu.HBM)


IN_VMEM = pl.BlockSpec(memory_space=pltpu.VMEM)
IN_HBM = pl.BlockSpec(memory_space=pltpu.HBM)


def call(body, shapes, args, flops, specs=None, scratch=(), limit=16 << 20):
    return pl.pallas_call(
        body,
        out_shape=shapes,
        in_specs=specs or [IN_VMEM] * len(args),
        out_specs=[IN_VMEM] * len(shapes),
        scratch_shapes=scratch,
        compiler_params=pltpu.CompilerParams(vmem_limit_bytes=limit),
        cost_estimate=pl.CostEstimate(flops=flops, bytes_accessed=0, transcendentals=0),
    )(*args)


def kept(shape, dtype):
    return pltpu.VMEM(shape, dtype)


def pairs(refs):
    values = [r[...].astype(F32) for r in refs]
    half = values[0].shape[0] // 2
    x_rows = jnp.concatenate([v[:half] for v in values], axis=0).astype(BF16)
    s_rows = jnp.concatenate([v[half:] for v in values], axis=0).astype(BF16)
    return x_rows, s_rows


def swap_half(value):
    halves = lax.axis_size("half")
    return lax.ppermute(value, "half", [(i, (i + 1) % halves) for i in range(halves)])


def small_program(activations, upstream, routes, gates, own, experts, capacity, hidden_units):
    batches, top, tokens_dev = routes.shape
    width = activations.shape[1]
    rows = batches * tokens_dev
    block = batches * capacity
    slots = experts * block
    units = own[0].shape[1]

    far = [swap_half(w) for w in own]

    def dispatch_body(x_hbm, u_hbm, routes_hbm, gates_hbm, *refs):
        *outs, pick_ref, data, routes_ref, gates_ref, sems = refs
        copies = [
            pltpu.make_async_copy(routes_hbm, routes_ref, sems.at[0]),
            pltpu.make_async_copy(gates_hbm, gates_ref, sems.at[1]),
            pltpu.make_async_copy(x_hbm, data.at[:rows], sems.at[2]),
            pltpu.make_async_copy(u_hbm, data.at[rows:], sems.at[3]),
        ]
        for copy in copies:
            copy.start()
        for copy in copies:
            copy.wait()
        sent, pick = route_rows(
            data[...],
            [routes_ref[m] for m in range(batches)],
            [gates_ref[m] for m in range(batches)],
            lax.axis_index("expert"), experts, capacity,
        )
        for d in range(experts):
            outs[d][...] = sent[2 * d * block : 2 * (d + 1) * block].astype(BF16)
        pick_ref[...] = pick

    *blocks, pick = call(
        dispatch_body,
        [kept((2 * block, width), BF16)] * experts + [kept((slots, rows), F32)],
        [hbm(v) for v in (activations, upstream, routes, gates)],
        10**7,
        specs=[IN_HBM] * 4,
        scratch=[
            pltpu.VMEM((2 * rows, width), BF16),
            pltpu.VMEM((batches, top, tokens_dev), jnp.int32),
            pltpu.VMEM((batches, top, tokens_dev), F32),
            pltpu.SemaphoreType.DMA((4,)),
        ],
    )

    def shift(value, by):
        return lax.ppermute(
            value, "expert", [(i, (i + by) % experts) for i in range(experts)]
        )

    blocks[-1], far[0] = lax.optimization_barrier((blocks[-1], far[0]))
    got = [blocks[0]] + [shift(blocks[d], d) for d in range(1, experts)]

    turned_shapes = [
        kept((units, width), BF16), kept((units, width), BF16), kept((width, units), BF16)
    ]

    def prepare_body(pick_ref, *refs):
        ins, far_refs, (gate, up), near_turned, far_turned, pick_out, down, sems = (
            refs[:3], refs[3:6], refs[6:8], refs[8:11], refs[11:14], *refs[14:]
        )
        held = (gate, up, down)
        copies = [pltpu.make_async_copy(ins[i], held[i], sems.at[i]) for i in range(3)]
        for copy in copies:
            copy.start()
        pick_out[...] = jnp.transpose(pick_ref[...]).astype(BF16)
        for source, to in zip(far_refs, far_turned):
            to[...] = jnp.transpose(source[...])
        for copy, source, to in zip(copies, held, near_turned):
            copy.wait()
            to[...] = jnp.transpose(source[...])

    gate, up, *turned, pick = call(
        prepare_body,
        [kept(w.shape, BF16) for w in own[:2]] + turned_shapes * 2 + [kept((rows, slots), BF16)],
        [vmem(pick)] + [hbm(w) for w in own] + [vmem(w) for w in far],
        10**9,
        specs=[IN_VMEM] + [IN_HBM] * 3 + [IN_VMEM] * 3,
        scratch=[pltpu.VMEM(own[2].shape, BF16), pltpu.SemaphoreType.DMA((3,))],
    )
    near, far = [gate, up, *turned[:3]], [*far[:2], *turned[3:]]

    def expert_body(*refs):
        held = [r[...] for r in refs[experts : experts + 10]]
        weights = [held[:5], held[5:]]
        to_other, mine, *outs = refs[experts + 10 :]
        x_rows, s_rows = pairs(refs[:experts])
        hidden, active, slope = forward_values(x_rows, weights)
        to_other[:, :units] = hidden[1]
        to_other[:, units : 2 * units] = hidden[0]
        to_other[:, 2 * units :] = s_rows
        mine[:, :units] = hidden[0]
        mine[:, units : 2 * units] = hidden[1]
        mine[:, 2 * units :] = s_rows
        total = backward_values(s_rows, active, slope, weights)
        for d in range(experts):
            outs[d][...] = total[d * block : (d + 1) * block].astype(BF16)

    to_other, mine, *grads = call(
        expert_body,
        [kept((slots, 2 * units + width), BF16)] * 2 + [kept((block, width), BF16)] * experts,
        [vmem(v) for v in (*got, *near, *far)],
        2 * slots * width * units * 10,
    )
    back = [grads[0]] + [shift(grads[d], experts - d) for d in range(1, experts)]
    theirs = swap_half(to_other)

    chunk = width // CHUNKS

    def core_body(mine_ref, theirs_ref, out_hbm, out_ref, sems):
        both = jnp.concatenate(
            [mine_ref[...].astype(F32), theirs_ref[...].astype(F32)], axis=0
        ).astype(BF16)
        mixed, rows_twice = polynomial_core(
            both[:, 2 * units :], both[:, : 2 * units], units, max(hidden_units, width)
        )
        copies = []
        for i in range(CHUNKS):
            cut = slice(i * chunk, (i + 1) * chunk)
            out_ref[:, cut] = plain(mixed, rows_twice[:, cut]).astype(BF16)
            copies.append(
                pltpu.make_async_copy(out_ref.at[:, cut], out_hbm.at[:, cut], sems.at[i])
            )
            copies[-1].start()
        for copy in copies:
            copy.wait()

    update = pl.pallas_call(
        core_body,
        out_shape=jax.ShapeDtypeStruct((units, width), BF16),
        in_specs=[IN_VMEM] * 2,
        out_specs=IN_HBM,
        scratch_shapes=[pltpu.VMEM((units, width), BF16), pltpu.SemaphoreType.DMA((CHUNKS,))],
        compiler_params=pltpu.CompilerParams(vmem_limit_bytes=16 << 20),
        cost_estimate=pl.CostEstimate(
            flops=2 * 4 * slots * width * units * 2, bytes_accessed=0, transcendentals=0
        ),
    )(vmem(mine), vmem(theirs))
    update, back = lax.optimization_barrier((update, back))

    def combine_body(pick_ref, *refs):
        rows_back = jnp.concatenate([r[...].astype(F32) for r in refs[:-1]], axis=0)
        refs[-1][...] = plain(pick_ref[...], rows_back.astype(BF16)).astype(BF16)

    (cotangent,) = call(
        combine_body,
        [jax.ShapeDtypeStruct((rows, width), BF16)],
        [vmem(pick)] + [vmem(b) for b in back],
        10**6,
    )
    return cotangent, update


def large_program(activations, upstream, routes, gates, own, experts, capacity, hidden_units):
    batches, top, tokens_dev = routes.shape
    width = activations.shape[1]
    block = batches * capacity
    slots = experts * block
    units = own[0].shape[1]
    sent, pick = route_rows(
        jnp.concatenate([activations, upstream], axis=0), routes, gates, 0, experts, capacity
    )
    weights = [(*w[:2], *(m.T for m in w)) for w in (own, [swap_half(w) for w in own])]
    sent = sent.astype(BF16).reshape(experts, 2 * block, width)
    got = lax.all_to_all(sent, "expert", split_axis=0, concat_axis=0, tiled=True)
    x_rows = got[:, :block].reshape(slots, width)
    s_rows = got[:, block:].reshape(slots, width)
    hidden, active, slope = forward_values(x_rows, weights)
    theirs = swap_half(jnp.concatenate([hidden[1], hidden[0], s_rows], axis=1))
    mine = jnp.concatenate([hidden[0], hidden[1], s_rows], axis=1)
    total = backward_values(s_rows, active, slope, weights)
    total = total.astype(BF16).reshape(experts, block, width)
    back = lax.all_to_all(total, "expert", split_axis=0, concat_axis=0, tiled=True)
    cotangent = dot(pick.astype(BF16), back.reshape(slots, width), ((0,), (0,))).astype(BF16)
    both = jnp.concatenate([mine, theirs], axis=0)
    mixed, rows_twice = polynomial_core(
        both[:, 2 * units :], both[:, : 2 * units], units, max(hidden_units, width)
    )
    return cotangent, plain(mixed, rows_twice).astype(BF16)


def on_device(activations, upstream, routes, route_gates, gate_matrix, up_matrix, down_matrix):
    experts = lax.axis_size("expert")
    halves = lax.axis_size("half")
    batches, tokens_dev, top = routes.shape
    width = activations.shape[2]
    capacity = max(2, 6 * tokens_dev * top // (5 * experts))
    rows = batches * tokens_dev
    own = (gate_matrix[0], up_matrix[0], down_matrix[0])
    hidden_units = down_matrix.shape[1] * halves
    program = small_program if experts <= MAX_PERMUTED else large_program
    cotangent, update = program(
        activations.reshape(rows, width),
        upstream.reshape(rows, width),
        jnp.swapaxes(routes, 1, 2),
        jnp.swapaxes(route_gates, 1, 2),
        own, experts, capacity, hidden_units,
    )
    return cotangent.reshape(batches, tokens_dev, width), update[None]


def solution(mesh):
    tokens = P(None, ("dp", "expert", "half"), None)
    return jax.shard_map(
        on_device,
        mesh=mesh,
        in_specs=(tokens,) * 4
        + (P("expert", None, "half"), P("expert", None, "half"), P("expert", "half", None)),
        out_specs=(tokens, P(("dp", "expert"), "half", None)),
        check_vma=False,
    )
```

```python
import functools
import math

import jax
import jax.numpy as jnp
from jax import lax
from jax.experimental import pallas as pl
from jax.experimental.pallas import tpu as pltpu
from jax.sharding import PartitionSpec as P

ITERS = 2
MAX_PERMUTED = 8
CHUNKS = 4

linear_term = 3.4445
cubic_term = -4.775
quintic_term = 2.0315

F32 = jnp.float32
BF16 = jnp.bfloat16


def dot(left, right, dims, precision=None):
    return lax.dot_general(
        left, right, (dims, ((), ())), precision=precision, preferred_element_type=F32
    )


def contract_last(left, right):
    return dot(left, right, ((1,), (1,)))


def plain(left, right, precision=None):
    return dot(left, right, ((1,), (0,)), precision)


def route_slots(routes, base, experts, block, capacity):
    tokens_dev = routes[0].shape[1]
    expert_ids = lax.broadcasted_iota(jnp.int32, (experts, tokens_dev), 0)
    row = lax.broadcasted_iota(jnp.int32, (tokens_dev, tokens_dev), 0)
    col = lax.broadcasted_iota(jnp.int32, (tokens_dev, tokens_dev), 1)
    earlier = jnp.where(row < col, 1.0, 0.0).astype(BF16)
    found = []
    for batch, named in enumerate(routes):
        top = named.shape[0]
        onehots = [jnp.where(named[k : k + 1] == expert_ids, 1.0, 0.0) for k in range(top)]
        before = plain(sum(onehots).astype(BF16), earlier)
        slots = []
        for k in range(top):
            position = jnp.sum(before * onehots[k], axis=0, keepdims=True).astype(jnp.int32)
            before = before + onehots[k]
            relative = named[k : k + 1] - base
            relative = jnp.where(relative < 0, relative + experts, relative)
            slots.append((relative, batch * capacity + position))
        found.append(slots)
    return found


def route_picks(routes, gates, base, experts, capacity):
    batches, top = len(routes), routes[0].shape[0]
    block = batches * capacity
    found = route_slots(routes, base, experts, block, capacity)
    joined = lambda rows: jnp.concatenate(rows, axis=1)
    tokens = batches * routes[0].shape[1]
    row = lax.broadcasted_iota(jnp.int32, (2 * experts * block, tokens), 0)
    slot = lax.broadcasted_iota(jnp.int32, (experts * block, tokens), 0)
    in_x = row[:, :1] % (2 * block) < block
    pick_x, pick_u, pick_tok, gate = 0.0, 0.0, 0.0, jnp.where(in_x, 1.0, 0.0)
    for k in range(top):
        relative = joined([found[m][k][0] for m in range(batches)])
        within = joined([found[m][k][1] for m in range(batches)])
        gates_k = joined([gates[m][k : k + 1] for m in range(batches)])
        at = relative * (2 * block) + within
        here = row == at + block
        pick_x = pick_x + jnp.where(row == at, 1.0, 0.0)
        pick_u = pick_u + jnp.where(here, 1.0, 0.0)
        pick_tok = pick_tok + jnp.where(slot == relative * block + within, 1.0, 0.0)
        gate = gate + jnp.sum(jnp.where(here, gates_k, 0.0), axis=1, keepdims=True)
    picks = joined([pick_x, pick_u]).astype(BF16)
    return picks, gate, pick_tok


def forward_values(x_rows, weights):
    hidden, active, slope = [], [], []
    for gate, up, *_ in weights:
        pre_gate = plain(x_rows, gate)
        pre_up = plain(x_rows, up)
        sigmoid = 1.0 / (1.0 + jnp.exp(-pre_gate))
        activated = pre_gate * sigmoid
        hidden.append((activated * pre_up).astype(BF16))
        active.append(activated)
        slope.append(pre_up * sigmoid * (1.0 + pre_gate * (1.0 - sigmoid)))
    return hidden, active, slope


def backward_values(s_rows, active, slope, weights):
    total = None
    for activated, steep, (_, _, gate_turned, up_turned, down_turned) in zip(
        active, slope, weights
    ):
        hidden_grad = plain(s_rows, down_turned)
        gate_grad = (hidden_grad * steep).astype(BF16)
        up_grad = (hidden_grad * activated).astype(BF16)
        piece = plain(gate_grad, gate_turned) + plain(up_grad, up_turned)
        piece = piece.astype(BF16).astype(F32)
        total = piece if total is None else total + piece
    return total


def parts_of(value, count):
    parts = []
    for _ in range(count):
        part = value.astype(BF16)
        parts.append(part)
        value = value - part.astype(F32)
    return parts


def product(left, right, count):
    terms = [
        plain(l, r)
        for i, l in enumerate(left)
        for j, r in enumerate(right)
        if i + j < count
    ]
    return sum(terms[1:], terms[0])


def polynomial_core(scaled, hidden, units, width):
    rows = scaled.shape[0]
    own = jnp.transpose(hidden[:, :units].astype(F32)).astype(BF16)
    left = contract_last(scaled, scaled)
    right = contract_last(hidden, hidden)
    squares = jnp.maximum(jnp.sum(left * right), 0.0)
    inverse = 1.0 / (jnp.sqrt(squares) + 1e-07)
    row = lax.broadcasted_iota(jnp.int32, (rows, rows), 0)
    col = lax.broadcasted_iota(jnp.int32, (rows, rows), 1)
    eye = jnp.where(row == col, linear_term, 0.0)
    moment = product(parts_of(left * inverse, 3), parts_of(right * inverse, 3), 3)
    mixed = [own]
    for iteration in range(ITERS):
        halves = parts_of(moment, 2)
        if iteration == ITERS - 1:
            once = product(mixed, halves, 2)
            twice = product(parts_of(once, 2), halves, 2)
            mixed = linear_term * sum(m.astype(F32) for m in mixed)
            mixed = mixed + cubic_term * once + quintic_term * twice
        else:
            factor = eye + cubic_term * moment + quintic_term * product(halves, halves, 2)
            factor = parts_of(factor, 2)
            mixed = parts_of(product(mixed, factor, 2), 2)
            moment = product(parts_of(product(halves, factor, 2), 2), factor, 2)
    high, low = parts_of(mixed * (inverse * math.sqrt(width)), 2)
    both = jnp.concatenate([high.astype(F32), low.astype(F32)], axis=1).astype(BF16)
    return both, jnp.concatenate([scaled, scaled], axis=0)


def vmem(value):
    return pltpu.with_memory_space_constraint(value, pltpu.VMEM)


def hbm(value):
    return pltpu.with_memory_space_constraint(value, pltpu.HBM)


IN_VMEM = pl.BlockSpec(memory_space=pltpu.VMEM)
IN_HBM = pl.BlockSpec(memory_space=pltpu.HBM)


def call(body, shapes, args, flops, specs=None, scratch=(), limit=16 << 20):
    return pl.pallas_call(
        body,
        out_shape=shapes,
        in_specs=specs or [IN_VMEM] * len(args),
        out_specs=[IN_VMEM] * len(shapes),
        scratch_shapes=scratch,
        compiler_params=pltpu.CompilerParams(vmem_limit_bytes=limit),
        cost_estimate=pl.CostEstimate(flops=flops, bytes_accessed=0, transcendentals=0),
    )(*args)


def kept(shape, dtype):
    return pltpu.VMEM(shape, dtype)


def pairs(refs):
    values = [r[...].astype(F32) for r in refs]
    half = values[0].shape[0] // 2
    x_rows = jnp.concatenate([v[:half] for v in values], axis=0).astype(BF16)
    s_rows = jnp.concatenate([v[half:] for v in values], axis=0).astype(BF16)
    return x_rows, s_rows


def swap_half(value):
    halves = lax.axis_size("half")
    return lax.ppermute(value, "half", [(i, (i + 1) % halves) for i in range(halves)])


def small_program(activations, upstream, routes, gates, own, experts, capacity, hidden_units):
    batches, top, tokens_dev = routes.shape
    width = activations.shape[1]
    rows = batches * tokens_dev
    block = batches * capacity
    slots = experts * block
    units = own[0].shape[1]

    far = [swap_half(w) for w in own]

    def dispatch_body(x_hbm, u_hbm, routes_hbm, gates_hbm, *refs):
        *outs, pick_ref, data, routes_ref, gates_ref, sems = refs
        copies = [
            pltpu.make_async_copy(routes_hbm, routes_ref, sems.at[0]),
            pltpu.make_async_copy(gates_hbm, gates_ref, sems.at[1]),
            pltpu.make_async_copy(x_hbm, data.at[:rows], sems.at[2]),
            pltpu.make_async_copy(u_hbm, data.at[rows:], sems.at[3]),
        ]
        for copy in copies:
            copy.start()
        for copy in copies[:2]:
            copy.wait()
        picks, gate, pick = route_picks(
            [routes_ref[m] for m in range(batches)],
            [gates_ref[m] for m in range(batches)],
            lax.axis_index("expert"), experts, capacity,
        )
        pick_ref[...] = pick
        for copy in copies[2:]:
            copy.wait()
        sent = plain(picks, data[...]) * gate
        for d in range(experts):
            outs[d][...] = sent[2 * d * block : 2 * (d + 1) * block].astype(BF16)

    *blocks, pick = call(
        dispatch_body,
        [kept((2 * block, width), BF16)] * experts + [kept((slots, rows), F32)],
        [hbm(v) for v in (activations, upstream, routes, gates)],
        10**7,
        specs=[IN_HBM] * 4,
        scratch=[
            pltpu.VMEM((2 * rows, width), BF16),
            pltpu.VMEM((batches, top, tokens_dev), jnp.int32),
            pltpu.VMEM((batches, top, tokens_dev), F32),
            pltpu.SemaphoreType.DMA((4,)),
        ],
    )

    def shift(value, by):
        return lax.ppermute(
            value, "expert", [(i, (i + by) % experts) for i in range(experts)]
        )

    blocks[1], far[0] = lax.optimization_barrier((blocks[1], far[0]))
    got = [shift(blocks[d], d) for d in range(experts - 1, 0, -1)]
    got = [blocks[0]] + got[::-1]

    turned_shapes = [
        kept((units, width), BF16), kept((units, width), BF16), kept((width, units), BF16)
    ]

    def prepare_body(pick_ref, *refs):
        ins, far_refs, (gate, up), near_turned, far_turned, pick_out, down, sems = (
            refs[:3], refs[3:6], refs[6:8], refs[8:11], refs[11:14], *refs[14:]
        )
        held = (gate, up, down)
        copies = [pltpu.make_async_copy(ins[i], held[i], sems.at[i]) for i in range(3)]
        for copy in copies:
            copy.start()
        pick_out[...] = jnp.transpose(pick_ref[...]).astype(BF16)
        for source, to in zip(far_refs, far_turned):
            to[...] = jnp.transpose(source[...])
        for copy, source, to in zip(copies, held, near_turned):
            copy.wait()
            to[...] = jnp.transpose(source[...])

    gate, up, *turned, pick = call(
        prepare_body,
        [kept(w.shape, BF16) for w in own[:2]] + turned_shapes * 2 + [kept((rows, slots), BF16)],
        [vmem(pick)] + [hbm(w) for w in own] + [vmem(w) for w in far],
        10**9,
        specs=[IN_VMEM] + [IN_HBM] * 3 + [IN_VMEM] * 3,
        scratch=[pltpu.VMEM(own[2].shape, BF16), pltpu.SemaphoreType.DMA((3,))],
    )
    near, far = [gate, up, *turned[:3]], [*far[:2], *turned[3:]]

    def expert_body(*refs):
        held = [r[...] for r in refs[experts : experts + 10]]
        weights = [held[:5], held[5:]]
        to_other, mine, *outs = refs[experts + 10 :]
        x_rows, s_rows = pairs(refs[:experts])
        hidden, active, slope = forward_values(x_rows, weights)
        to_other[:, :units] = hidden[1]
        to_other[:, units : 2 * units] = hidden[0]
        to_other[:, 2 * units :] = s_rows
        mine[:, :units] = hidden[0]
        mine[:, units : 2 * units] = hidden[1]
        mine[:, 2 * units :] = s_rows
        total = backward_values(s_rows, active, slope, weights)
        for d in range(experts):
            outs[d][...] = total[d * block : (d + 1) * block].astype(BF16)

    to_other, mine, *grads = call(
        expert_body,
        [kept((slots, 2 * units + width), BF16)] * 2 + [kept((block, width), BF16)] * experts,
        [vmem(v) for v in (*got, *near, *far)],
        2 * slots * width * units * 10,
    )
    back = [grads[0]] + [shift(grads[d], experts - d) for d in range(1, experts)]
    theirs = swap_half(to_other)

    chunk = width // CHUNKS

    def core_body(mine_ref, theirs_ref, out_hbm, out_ref, sems):
        both = jnp.concatenate(
            [mine_ref[...].astype(F32), theirs_ref[...].astype(F32)], axis=0
        ).astype(BF16)
        mixed, rows_twice = polynomial_core(
            both[:, 2 * units :], both[:, : 2 * units], units, max(hidden_units, width)
        )
        copies = []
        for i in range(CHUNKS):
            cut = slice(i * chunk, (i + 1) * chunk)
            out_ref[:, cut] = plain(mixed, rows_twice[:, cut]).astype(BF16)
            copies.append(
                pltpu.make_async_copy(out_ref.at[:, cut], out_hbm.at[:, cut], sems.at[i])
            )
            copies[-1].start()
        for copy in copies:
            copy.wait()

    update = pl.pallas_call(
        core_body,
        out_shape=jax.ShapeDtypeStruct((units, width), BF16),
        in_specs=[IN_VMEM] * 2,
        out_specs=IN_HBM,
        scratch_shapes=[pltpu.VMEM((units, width), BF16), pltpu.SemaphoreType.DMA((CHUNKS,))],
        compiler_params=pltpu.CompilerParams(vmem_limit_bytes=16 << 20),
        cost_estimate=pl.CostEstimate(
            flops=2 * 4 * slots * width * units * 2, bytes_accessed=0, transcendentals=0
        ),
    )(vmem(mine), vmem(theirs))
    update, back = lax.optimization_barrier((update, back))

    def combine_body(pick_ref, *refs):
        rows_back = jnp.concatenate([r[...].astype(F32) for r in refs[:-1]], axis=0)
        refs[-1][...] = plain(pick_ref[...], rows_back.astype(BF16)).astype(BF16)

    (cotangent,) = call(
        combine_body,
        [jax.ShapeDtypeStruct((rows, width), BF16)],
        [vmem(pick)] + [vmem(b) for b in back],
        10**6,
    )
    return cotangent, update


def large_program(activations, upstream, routes, gates, own, experts, capacity, hidden_units):
    batches, top, tokens_dev = routes.shape
    width = activations.shape[1]
    block = batches * capacity
    slots = experts * block
    units = own[0].shape[1]
    picks, gate, pick = route_picks(routes, gates, 0, experts, capacity)
    sent = plain(picks, jnp.concatenate([activations, upstream], axis=0)) * gate
    weights = [(*w[:2], *(m.T for m in w)) for w in (own, [swap_half(w) for w in own])]
    sent = sent.astype(BF16).reshape(experts, 2 * block, width)
    got = lax.all_to_all(sent, "expert", split_axis=0, concat_axis=0, tiled=True)
    x_rows = got[:, :block].reshape(slots, width)
    s_rows = got[:, block:].reshape(slots, width)
    hidden, active, slope = forward_values(x_rows, weights)
    theirs = swap_half(jnp.concatenate([hidden[1], hidden[0], s_rows], axis=1))
    mine = jnp.concatenate([hidden[0], hidden[1], s_rows], axis=1)
    total = backward_values(s_rows, active, slope, weights)
    total = total.astype(BF16).reshape(experts, block, width)
    back = lax.all_to_all(total, "expert", split_axis=0, concat_axis=0, tiled=True)
    cotangent = dot(pick.astype(BF16), back.reshape(slots, width), ((0,), (0,))).astype(BF16)
    both = jnp.concatenate([mine, theirs], axis=0)
    mixed, rows_twice = polynomial_core(
        both[:, 2 * units :], both[:, : 2 * units], units, max(hidden_units, width)
    )
    return cotangent, plain(mixed, rows_twice).astype(BF16)


def on_device(activations, upstream, routes, route_gates, gate_matrix, up_matrix, down_matrix):
    experts = lax.axis_size("expert")
    halves = lax.axis_size("half")
    batches, tokens_dev, top = routes.shape
    width = activations.shape[2]
    capacity = max(2, 6 * tokens_dev * top // (5 * experts))
    rows = batches * tokens_dev
    own = (gate_matrix[0], up_matrix[0], down_matrix[0])
    hidden_units = down_matrix.shape[1] * halves
    program = small_program if experts <= MAX_PERMUTED else large_program
    cotangent, update = program(
        activations.reshape(rows, width),
        upstream.reshape(rows, width),
        jnp.swapaxes(routes, 1, 2),
        jnp.swapaxes(route_gates, 1, 2),
        own, experts, capacity, hidden_units,
    )
    return cotangent.reshape(batches, tokens_dev, width), update[None]


def solution(mesh):
    tokens = P(None, ("dp", "expert", "half"), None)
    return jax.shard_map(
        on_device,
        mesh=mesh,
        in_specs=(tokens,) * 4
        + (P("expert", None, "half"), P("expert", None, "half"), P("expert", "half", None)),
        out_specs=(tokens, P(("dp", "expert"), "half", None)),
        check_vma=False,
    )
```

```python
import functools
import math

import jax
import jax.numpy as jnp
from jax import lax
from jax.experimental import pallas as pl
from jax.experimental.pallas import tpu as pltpu
from jax.sharding import PartitionSpec as P

ITERS = 2
MAX_PERMUTED = 8
CHUNKS = 4

linear_term = 3.4445
cubic_term = -4.775
quintic_term = 2.0315

F32 = jnp.float32
BF16 = jnp.bfloat16


def dot(left, right, dims, precision=None):
    return lax.dot_general(
        left, right, (dims, ((), ())), precision=precision, preferred_element_type=F32
    )


def contract_last(left, right):
    return dot(left, right, ((1,), (1,)))


def plain(left, right, precision=None):
    return dot(left, right, ((1,), (0,)), precision)


def route_slots(routes, base, experts, block, capacity):
    tokens_dev = routes[0].shape[1]
    expert_ids = lax.broadcasted_iota(jnp.int32, (experts, tokens_dev), 0)
    row = lax.broadcasted_iota(jnp.int32, (tokens_dev, tokens_dev), 0)
    col = lax.broadcasted_iota(jnp.int32, (tokens_dev, tokens_dev), 1)
    earlier = jnp.where(row < col, 1.0, 0.0).astype(BF16)
    found = []
    for batch, named in enumerate(routes):
        top = named.shape[0]
        onehots = [jnp.where(named[k : k + 1] == expert_ids, 1.0, 0.0) for k in range(top)]
        before = plain(sum(onehots).astype(BF16), earlier)
        slots = []
        for k in range(top):
            position = jnp.sum(before * onehots[k], axis=0, keepdims=True).astype(jnp.int32)
            before = before + onehots[k]
            relative = named[k : k + 1] - base
            relative = jnp.where(relative < 0, relative + experts, relative)
            slots.append((relative, batch * capacity + position))
        found.append(slots)
    return found


def route_picks(routes, gates, base, experts, capacity):
    batches, top = len(routes), routes[0].shape[0]
    block = batches * capacity
    found = route_slots(routes, base, experts, block, capacity)
    joined = lambda rows: jnp.concatenate(rows, axis=1)
    tokens = batches * routes[0].shape[1]
    row = lax.broadcasted_iota(jnp.int32, (2 * experts * block, tokens), 0)
    slot = lax.broadcasted_iota(jnp.int32, (experts * block, tokens), 0)
    in_x = row[:, :1] % (2 * block) < block
    pick_x, pick_u, pick_tok, gate = 0.0, 0.0, 0.0, jnp.where(in_x, 1.0, 0.0)
    for k in range(top):
        relative = joined([found[m][k][0] for m in range(batches)])
        within = joined([found[m][k][1] for m in range(batches)])
        gates_k = joined([gates[m][k : k + 1] for m in range(batches)])
        at = relative * (2 * block) + within
        here = row == at + block
        pick_x = pick_x + jnp.where(row == at, 1.0, 0.0)
        pick_u = pick_u + jnp.where(here, 1.0, 0.0)
        pick_tok = pick_tok + jnp.where(slot == relative * block + within, 1.0, 0.0)
        gate = gate + jnp.sum(jnp.where(here, gates_k, 0.0), axis=1, keepdims=True)
    picks = joined([pick_x, pick_u]).astype(BF16)
    return picks, gate, pick_tok


def forward_values(x_rows, weights):
    hidden, active, slope = [], [], []
    for gate, up, *_ in weights:
        pre_gate = plain(x_rows, gate)
        pre_up = plain(x_rows, up)
        sigmoid = 1.0 / (1.0 + jnp.exp(-pre_gate))
        activated = pre_gate * sigmoid
        hidden.append((activated * pre_up).astype(BF16))
        active.append(activated)
        slope.append(pre_up * sigmoid * (1.0 + pre_gate * (1.0 - sigmoid)))
    return hidden, active, slope


def backward_values(s_rows, active, slope, weights):
    total = None
    for activated, steep, (_, _, gate_turned, up_turned, down_turned) in zip(
        active, slope, weights
    ):
        hidden_grad = plain(s_rows, down_turned)
        gate_grad = (hidden_grad * steep).astype(BF16)
        up_grad = (hidden_grad * activated).astype(BF16)
        piece = plain(gate_grad, gate_turned) + plain(up_grad, up_turned)
        piece = piece.astype(BF16).astype(F32)
        total = piece if total is None else total + piece
    return total


def parts_of(value, count):
    parts = []
    for _ in range(count):
        part = value.astype(BF16)
        parts.append(part)
        value = value - part.astype(F32)
    return parts


def product(left, right, count):
    terms = [
        plain(l, r)
        for i, l in enumerate(left)
        for j, r in enumerate(right)
        if i + j < count
    ]
    return sum(terms[1:], terms[0])


def polynomial_core(scaled, hidden, units, width):
    rows = scaled.shape[0]
    own = jnp.transpose(hidden[:, :units].astype(F32)).astype(BF16)
    left = contract_last(scaled, scaled)
    right = contract_last(hidden, hidden)
    squares = jnp.maximum(jnp.sum(left * right), 0.0)
    inverse = 1.0 / (jnp.sqrt(squares) + 1e-07)
    row = lax.broadcasted_iota(jnp.int32, (rows, rows), 0)
    col = lax.broadcasted_iota(jnp.int32, (rows, rows), 1)
    eye = jnp.where(row == col, linear_term, 0.0)
    moment = product(parts_of(left * inverse, 3), parts_of(right * inverse, 3), 3)
    mixed = [own]
    for iteration in range(ITERS):
        halves = parts_of(moment, 2)
        if iteration == ITERS - 1:
            once = product(mixed, halves, 2)
            twice = product(parts_of(once, 2), halves, 2)
            mixed = linear_term * sum(m.astype(F32) for m in mixed)
            mixed = mixed + cubic_term * once + quintic_term * twice
        else:
            factor = eye + cubic_term * moment + quintic_term * product(halves, halves, 2)
            factor = parts_of(factor, 2)
            mixed = parts_of(product(mixed, factor, 2), 2)
            moment = product(parts_of(product(halves, factor, 2), 2), factor, 2)
    high, low = parts_of(mixed * (inverse * math.sqrt(width)), 2)
    both = jnp.concatenate([high.astype(F32), low.astype(F32)], axis=1).astype(BF16)
    return both, jnp.concatenate([scaled, scaled], axis=0)


def vmem(value):
    return pltpu.with_memory_space_constraint(value, pltpu.VMEM)


def hbm(value):
    return pltpu.with_memory_space_constraint(value, pltpu.HBM)


IN_VMEM = pl.BlockSpec(memory_space=pltpu.VMEM)
IN_HBM = pl.BlockSpec(memory_space=pltpu.HBM)


def call(body, shapes, args, flops, specs=None, scratch=(), limit=16 << 20):
    return pl.pallas_call(
        body,
        out_shape=shapes,
        in_specs=specs or [IN_VMEM] * len(args),
        out_specs=[IN_VMEM] * len(shapes),
        scratch_shapes=scratch,
        compiler_params=pltpu.CompilerParams(vmem_limit_bytes=limit),
        cost_estimate=pl.CostEstimate(flops=flops, bytes_accessed=0, transcendentals=0),
    )(*args)


def kept(shape, dtype):
    return pltpu.VMEM(shape, dtype)


def pairs(refs):
    values = [r[...].astype(F32) for r in refs]
    half = values[0].shape[0] // 2
    x_rows = jnp.concatenate([v[:half] for v in values], axis=0).astype(BF16)
    s_rows = jnp.concatenate([v[half:] for v in values], axis=0).astype(BF16)
    return x_rows, s_rows


def swap_half(value):
    halves = lax.axis_size("half")
    return lax.ppermute(value, "half", [(i, (i + 1) % halves) for i in range(halves)])


def small_program(activations, upstream, routes, gates, own, experts, capacity, hidden_units):
    batches, top, tokens_dev = routes.shape
    width = activations.shape[1]
    rows = batches * tokens_dev
    block = batches * capacity
    slots = experts * block
    units = own[0].shape[1]

    far = [swap_half(w) for w in own]

    def dispatch_body(x_hbm, u_hbm, routes_hbm, gates_hbm, *refs):
        *outs, pick_ref, data, routes_ref, gates_ref, sems = refs
        copies = [
            pltpu.make_async_copy(routes_hbm, routes_ref, sems.at[0]),
            pltpu.make_async_copy(gates_hbm, gates_ref, sems.at[1]),
            pltpu.make_async_copy(x_hbm, data.at[:rows], sems.at[2]),
            pltpu.make_async_copy(u_hbm, data.at[rows:], sems.at[3]),
        ]
        for copy in copies:
            copy.start()
        for copy in copies[:2]:
            copy.wait()
        picks, gate, pick = route_picks(
            [routes_ref[m] for m in range(batches)],
            [gates_ref[m] for m in range(batches)],
            lax.axis_index("expert"), experts, capacity,
        )
        pick_ref[...] = pick
        for copy in copies[2:]:
            copy.wait()
        sent = plain(picks, data[...]) * gate
        for d in range(experts):
            outs[d][...] = sent[2 * d * block : 2 * (d + 1) * block].astype(BF16)

    *blocks, pick = call(
        dispatch_body,
        [kept((2 * block, width), BF16)] * experts + [kept((slots, rows), F32)],
        [hbm(v) for v in (activations, upstream, routes, gates)],
        10**7,
        specs=[IN_HBM] * 4,
        scratch=[
            pltpu.VMEM((2 * rows, width), BF16),
            pltpu.VMEM((batches, top, tokens_dev), jnp.int32),
            pltpu.VMEM((batches, top, tokens_dev), F32),
            pltpu.SemaphoreType.DMA((4,)),
        ],
    )

    def shift(value, by):
        halves = lax.axis_size("half")
        pairs = [
            (i * halves + h, (i + by) % experts * halves + halves - 1 - h)
            for i in range(experts)
            for h in range(halves)
        ]
        return lax.ppermute(value, ("expert", "half"), pairs)

    blocks[1], far[0] = lax.optimization_barrier((blocks[1], far[0]))
    got = [shift(blocks[d], d) for d in range(experts - 1, 0, -1)]
    got = [blocks[0]] + got[::-1]

    turned_shapes = [
        kept((units, width), BF16), kept((units, width), BF16), kept((width, units), BF16)
    ]

    def prepare_body(pick_ref, *refs):
        ins, far_refs, (gate, up), near_turned, far_turned, pick_out, down, sems = (
            refs[:3], refs[3:6], refs[6:8], refs[8:11], refs[11:14], *refs[14:]
        )
        held = (gate, up, down)
        copies = [pltpu.make_async_copy(ins[i], held[i], sems.at[i]) for i in range(3)]
        for copy in copies:
            copy.start()
        pick_out[...] = jnp.transpose(pick_ref[...]).astype(BF16)
        for source, to in zip(far_refs, far_turned):
            to[...] = jnp.transpose(source[...])
        for copy, source, to in zip(copies, held, near_turned):
            copy.wait()
            to[...] = jnp.transpose(source[...])

    gate, up, *turned, pick = call(
        prepare_body,
        [kept(w.shape, BF16) for w in own[:2]] + turned_shapes * 2 + [kept((rows, slots), BF16)],
        [vmem(pick)] + [hbm(w) for w in own] + [vmem(w) for w in far],
        10**9,
        specs=[IN_VMEM] + [IN_HBM] * 3 + [IN_VMEM] * 3,
        scratch=[pltpu.VMEM(own[2].shape, BF16), pltpu.SemaphoreType.DMA((3,))],
    )
    near, far = [gate, up, *turned[:3]], [*far[:2], *turned[3:]]

    def expert_body(*refs):
        held = [r[...] for r in refs[experts : experts + 10]]
        weights = [held[:5], held[5:]]
        to_other, mine, *outs = refs[experts + 10 :]
        x_rows, s_rows = pairs(refs[:experts])
        hidden, active, slope = forward_values(x_rows, weights)
        to_other[:, :units] = hidden[1]
        to_other[:, units : 2 * units] = hidden[0]
        to_other[:, 2 * units :] = s_rows
        mine[:, :units] = hidden[0]
        mine[:, units : 2 * units] = hidden[1]
        mine[:, 2 * units :] = s_rows
        total = backward_values(s_rows, active, slope, weights)
        for d in range(experts):
            outs[d][...] = total[d * block : (d + 1) * block].astype(BF16)

    to_other, mine, *grads = call(
        expert_body,
        [kept((slots, 2 * units + width), BF16)] * 2 + [kept((block, width), BF16)] * experts,
        [vmem(v) for v in (*got, *near, *far)],
        2 * slots * width * units * 10,
    )
    back = [grads[0]] + [shift(grads[d], experts - d) for d in range(1, experts)]
    theirs = swap_half(to_other)

    chunk = width // CHUNKS

    def core_body(mine_ref, theirs_ref, out_hbm, out_ref, sems):
        both = jnp.concatenate(
            [mine_ref[...].astype(F32), theirs_ref[...].astype(F32)], axis=0
        ).astype(BF16)
        mixed, rows_twice = polynomial_core(
            both[:, 2 * units :], both[:, : 2 * units], units, max(hidden_units, width)
        )
        copies = []
        for i in range(CHUNKS):
            cut = slice(i * chunk, (i + 1) * chunk)
            out_ref[:, cut] = plain(mixed, rows_twice[:, cut]).astype(BF16)
            copies.append(
                pltpu.make_async_copy(out_ref.at[:, cut], out_hbm.at[:, cut], sems.at[i])
            )
            copies[-1].start()
        for copy in copies:
            copy.wait()

    update = pl.pallas_call(
        core_body,
        out_shape=jax.ShapeDtypeStruct((units, width), BF16),
        in_specs=[IN_VMEM] * 2,
        out_specs=IN_HBM,
        scratch_shapes=[pltpu.VMEM((units, width), BF16), pltpu.SemaphoreType.DMA((CHUNKS,))],
        compiler_params=pltpu.CompilerParams(vmem_limit_bytes=16 << 20),
        cost_estimate=pl.CostEstimate(
            flops=2 * 4 * slots * width * units * 2, bytes_accessed=0, transcendentals=0
        ),
    )(vmem(mine), vmem(theirs))
    update, back = lax.optimization_barrier((update, back))

    def combine_body(pick_ref, *refs):
        rows_back = jnp.concatenate([r[...].astype(F32) for r in refs[:-1]], axis=0)
        refs[-1][...] = plain(pick_ref[...], rows_back.astype(BF16)).astype(BF16)

    (cotangent,) = call(
        combine_body,
        [jax.ShapeDtypeStruct((rows, width), BF16)],
        [vmem(pick)] + [vmem(b) for b in back],
        10**6,
    )
    return cotangent, update


def large_program(activations, upstream, routes, gates, own, experts, capacity, hidden_units):
    batches, top, tokens_dev = routes.shape
    width = activations.shape[1]
    block = batches * capacity
    slots = experts * block
    units = own[0].shape[1]
    picks, gate, pick = route_picks(routes, gates, 0, experts, capacity)
    sent = plain(picks, jnp.concatenate([activations, upstream], axis=0)) * gate
    weights = [(*w[:2], *(m.T for m in w)) for w in (own, [swap_half(w) for w in own])]
    sent = sent.astype(BF16).reshape(experts, 2 * block, width)
    got = lax.all_to_all(sent, "expert", split_axis=0, concat_axis=0, tiled=True)
    x_rows = got[:, :block].reshape(slots, width)
    s_rows = got[:, block:].reshape(slots, width)
    hidden, active, slope = forward_values(x_rows, weights)
    theirs = swap_half(jnp.concatenate([hidden[1], hidden[0], s_rows], axis=1))
    mine = jnp.concatenate([hidden[0], hidden[1], s_rows], axis=1)
    total = backward_values(s_rows, active, slope, weights)
    total = total.astype(BF16).reshape(experts, block, width)
    back = lax.all_to_all(total, "expert", split_axis=0, concat_axis=0, tiled=True)
    cotangent = dot(pick.astype(BF16), back.reshape(slots, width), ((0,), (0,))).astype(BF16)
    both = jnp.concatenate([mine, theirs], axis=0)
    mixed, rows_twice = polynomial_core(
        both[:, 2 * units :], both[:, : 2 * units], units, max(hidden_units, width)
    )
    return cotangent, plain(mixed, rows_twice).astype(BF16)


def on_device(activations, upstream, routes, route_gates, gate_matrix, up_matrix, down_matrix):
    experts = lax.axis_size("expert")
    halves = lax.axis_size("half")
    batches, tokens_dev, top = routes.shape
    width = activations.shape[2]
    capacity = max(2, 6 * tokens_dev * top // (5 * experts))
    rows = batches * tokens_dev
    own = (gate_matrix[0], up_matrix[0], down_matrix[0])
    hidden_units = down_matrix.shape[1] * halves
    program = small_program if experts <= MAX_PERMUTED else large_program
    cotangent, update = program(
        activations.reshape(rows, width),
        upstream.reshape(rows, width),
        jnp.swapaxes(routes, 1, 2),
        jnp.swapaxes(route_gates, 1, 2),
        own, experts, capacity, hidden_units,
    )
    return cotangent.reshape(batches, tokens_dev, width), update[None]


def solution(mesh):
    tokens = P(None, ("dp", "expert", "half"), None)
    return jax.shard_map(
        on_device,
        mesh=mesh,
        in_specs=(tokens,) * 4
        + (P("expert", None, "half"), P("expert", None, "half"), P("expert", "half", None)),
        out_specs=(tokens, P(("dp", "expert"), "half", None)),
        check_vma=False,
    )
```

```python
import functools
import math

import jax
import jax.numpy as jnp
from jax import lax
from jax.experimental import pallas as pl
from jax.experimental.pallas import tpu as pltpu
from jax.sharding import PartitionSpec as P

ITERS = 2
MAX_PERMUTED = 8
CHUNKS = 4

linear_term = 3.4445
cubic_term = -4.775
quintic_term = 2.0315

F32 = jnp.float32
BF16 = jnp.bfloat16


def dot(left, right, dims, precision=None):
    return lax.dot_general(
        left, right, (dims, ((), ())), precision=precision, preferred_element_type=F32
    )


def contract_last(left, right):
    return dot(left, right, ((1,), (1,)))


def plain(left, right, precision=None):
    return dot(left, right, ((1,), (0,)), precision)


def route_slots(routes, base, experts, block, capacity):
    tokens_dev = routes[0].shape[1]
    expert_ids = lax.broadcasted_iota(jnp.int32, (experts, tokens_dev), 0)
    row = lax.broadcasted_iota(jnp.int32, (tokens_dev, tokens_dev), 0)
    col = lax.broadcasted_iota(jnp.int32, (tokens_dev, tokens_dev), 1)
    earlier = jnp.where(row < col, 1.0, 0.0).astype(BF16)
    found = []
    for batch, named in enumerate(routes):
        top = named.shape[0]
        onehots = [jnp.where(named[k : k + 1] == expert_ids, 1.0, 0.0) for k in range(top)]
        before = plain(sum(onehots).astype(BF16), earlier)
        slots = []
        for k in range(top):
            position = jnp.sum(before * onehots[k], axis=0, keepdims=True).astype(jnp.int32)
            before = before + onehots[k]
            relative = named[k : k + 1] - base
            relative = jnp.where(relative < 0, relative + experts, relative)
            slots.append((relative, batch * capacity + position))
        found.append(slots)
    return found


def ring_place(expert, experts):
    back = jnp.where(expert == 0, 0, experts - expert // 2)
    return jnp.where(expert % 2 == 1, (expert + 1) // 2, back)


def ring_order(experts):
    return [0, *range(1, experts, 2), *reversed(range(2, experts, 2))]


def route_picks(routes, gates, base, experts, capacity):
    batches, top = len(routes), routes[0].shape[0]
    block = batches * capacity
    found = route_slots(routes, base, experts, block, capacity)
    joined = lambda rows: jnp.concatenate(rows, axis=1)
    tokens = batches * routes[0].shape[1]
    row = lax.broadcasted_iota(jnp.int32, (2 * experts * block, tokens), 0)
    slot = lax.broadcasted_iota(jnp.int32, (experts * block, tokens), 0)
    in_x = row[:, :1] % (2 * block) < block
    pick_x, pick_u, pick_tok, gate = 0.0, 0.0, 0.0, jnp.where(in_x, 1.0, 0.0)
    for k in range(top):
        relative = joined([found[m][k][0] for m in range(batches)])
        within = joined([found[m][k][1] for m in range(batches)])
        gates_k = joined([gates[m][k : k + 1] for m in range(batches)])
        at = relative * (2 * block) + within
        here = row == at + block
        pick_x = pick_x + jnp.where(row == at, 1.0, 0.0)
        pick_u = pick_u + jnp.where(here, 1.0, 0.0)
        pick_tok = pick_tok + jnp.where(slot == relative * block + within, 1.0, 0.0)
        gate = gate + jnp.sum(jnp.where(here, gates_k, 0.0), axis=1, keepdims=True)
    picks = joined([pick_x, pick_u]).astype(BF16)
    return picks, gate, pick_tok


def forward_values(x_rows, weights):
    hidden, active, slope = [], [], []
    for gate, up, *_ in weights:
        pre_gate = plain(x_rows, gate)
        pre_up = plain(x_rows, up)
        sigmoid = 1.0 / (1.0 + jnp.exp(-pre_gate))
        activated = pre_gate * sigmoid
        hidden.append((activated * pre_up).astype(BF16))
        active.append(activated)
        slope.append(pre_up * sigmoid * (1.0 + pre_gate * (1.0 - sigmoid)))
    return hidden, active, slope


def backward_values(s_rows, active, slope, weights):
    total = None
    for activated, steep, (_, _, gate_turned, up_turned, down_turned) in zip(
        active, slope, weights
    ):
        hidden_grad = plain(s_rows, down_turned)
        gate_grad = (hidden_grad * steep).astype(BF16)
        up_grad = (hidden_grad * activated).astype(BF16)
        piece = plain(gate_grad, gate_turned) + plain(up_grad, up_turned)
        piece = piece.astype(BF16).astype(F32)
        total = piece if total is None else total + piece
    return total


def parts_of(value, count):
    parts = []
    for _ in range(count):
        part = value.astype(BF16)
        parts.append(part)
        value = value - part.astype(F32)
    return parts


def product(left, right, count):
    terms = [
        plain(l, r)
        for i, l in enumerate(left)
        for j, r in enumerate(right)
        if i + j < count
    ]
    return sum(terms[1:], terms[0])


def polynomial_core(scaled, hidden, units, width):
    rows = scaled.shape[0]
    own = jnp.transpose(hidden[:, :units].astype(F32)).astype(BF16)
    left = contract_last(scaled, scaled)
    right = contract_last(hidden, hidden)
    squares = jnp.maximum(jnp.sum(left * right), 0.0)
    inverse = 1.0 / (jnp.sqrt(squares) + 1e-07)
    row = lax.broadcasted_iota(jnp.int32, (rows, rows), 0)
    col = lax.broadcasted_iota(jnp.int32, (rows, rows), 1)
    eye = jnp.where(row == col, linear_term, 0.0)
    moment = product(parts_of(left * inverse, 3), parts_of(right * inverse, 3), 3)
    mixed = [own]
    for iteration in range(ITERS):
        halves = parts_of(moment, 2)
        if iteration == ITERS - 1:
            once = product(mixed, halves, 2)
            twice = product(parts_of(once, 2), halves, 2)
            mixed = linear_term * sum(m.astype(F32) for m in mixed)
            mixed = mixed + cubic_term * once + quintic_term * twice
        else:
            factor = eye + cubic_term * moment + quintic_term * product(halves, halves, 2)
            factor = parts_of(factor, 2)
            mixed = parts_of(product(mixed, factor, 2), 2)
            moment = product(parts_of(product(halves, factor, 2), 2), factor, 2)
    high, low = parts_of(mixed * (inverse * math.sqrt(width)), 2)
    both = jnp.concatenate([high.astype(F32), low.astype(F32)], axis=1).astype(BF16)
    return both, jnp.concatenate([scaled, scaled], axis=0)


def vmem(value):
    return pltpu.with_memory_space_constraint(value, pltpu.VMEM)


def hbm(value):
    return pltpu.with_memory_space_constraint(value, pltpu.HBM)


IN_VMEM = pl.BlockSpec(memory_space=pltpu.VMEM)
IN_HBM = pl.BlockSpec(memory_space=pltpu.HBM)


def call(body, shapes, args, flops, specs=None, scratch=(), limit=16 << 20):
    return pl.pallas_call(
        body,
        out_shape=shapes,
        in_specs=specs or [IN_VMEM] * len(args),
        out_specs=[IN_VMEM] * len(shapes),
        scratch_shapes=scratch,
        compiler_params=pltpu.CompilerParams(vmem_limit_bytes=limit),
        cost_estimate=pl.CostEstimate(flops=flops, bytes_accessed=0, transcendentals=0),
    )(*args)


def kept(shape, dtype):
    return pltpu.VMEM(shape, dtype)


def pairs(refs):
    values = [r[...].astype(F32) for r in refs]
    half = values[0].shape[0] // 2
    x_rows = jnp.concatenate([v[:half] for v in values], axis=0).astype(BF16)
    s_rows = jnp.concatenate([v[half:] for v in values], axis=0).astype(BF16)
    return x_rows, s_rows


def swap_half(value):
    halves = lax.axis_size("half")
    return lax.ppermute(value, "half", [(i, (i + 1) % halves) for i in range(halves)])


def small_program(activations, upstream, routes, gates, own, experts, capacity, hidden_units):
    batches, top, tokens_dev = routes.shape
    width = activations.shape[1]
    rows = batches * tokens_dev
    block = batches * capacity
    slots = experts * block
    units = own[0].shape[1]

    far = [swap_half(w) for w in own]

    def dispatch_body(x_hbm, u_hbm, routes_hbm, gates_hbm, *refs):
        *outs, pick_ref, data, routes_ref, gates_ref, sems = refs
        copies = [
            pltpu.make_async_copy(routes_hbm, routes_ref, sems.at[0]),
            pltpu.make_async_copy(gates_hbm, gates_ref, sems.at[1]),
            pltpu.make_async_copy(x_hbm, data.at[:rows], sems.at[2]),
            pltpu.make_async_copy(u_hbm, data.at[rows:], sems.at[3]),
        ]
        for copy in copies:
            copy.start()
        for copy in copies[:2]:
            copy.wait()
        picks, gate, pick = route_picks(
            [ring_place(routes_ref[m], experts) for m in range(batches)],
            [gates_ref[m] for m in range(batches)],
            ring_place(lax.axis_index("expert"), experts), experts, capacity,
        )
        pick_ref[...] = pick
        for copy in copies[2:]:
            copy.wait()
        sent = plain(picks, data[...]) * gate
        for d in range(experts):
            outs[d][...] = sent[2 * d * block : 2 * (d + 1) * block].astype(BF16)

    *blocks, pick = call(
        dispatch_body,
        [kept((2 * block, width), BF16)] * experts + [kept((slots, rows), F32)],
        [hbm(v) for v in (activations, upstream, routes, gates)],
        10**7,
        specs=[IN_HBM] * 4,
        scratch=[
            pltpu.VMEM((2 * rows, width), BF16),
            pltpu.VMEM((batches, top, tokens_dev), jnp.int32),
            pltpu.VMEM((batches, top, tokens_dev), F32),
            pltpu.SemaphoreType.DMA((4,)),
        ],
    )

    def shift(value, by):
        halves = lax.axis_size("half")
        ring = ring_order(experts)
        pairs = [
            (ring[i] * halves + h, ring[(i + by) % experts] * halves + halves - 1 - h)
            for i in range(experts)
            for h in range(halves)
        ]
        return lax.ppermute(value, ("expert", "half"), pairs)

    middle = experts // 2
    order = [*range(max(1, middle), experts), *range(middle - 1, 0, -1)]
    if order:
        last = order[-1]
        blocks[last], far[0] = lax.optimization_barrier((blocks[last], far[0]))
    got = list(blocks)
    for d in order:
        got[d] = shift(blocks[d], d)

    turned_shapes = [
        kept((units, width), BF16), kept((units, width), BF16), kept((width, units), BF16)
    ]

    def prepare_body(pick_ref, *refs):
        ins, far_refs, (gate, up), near_turned, far_turned, pick_out, down, sems = (
            refs[:3], refs[3:6], refs[6:8], refs[8:11], refs[11:14], *refs[14:]
        )
        held = (gate, up, down)
        copies = [pltpu.make_async_copy(ins[i], held[i], sems.at[i]) for i in range(3)]
        for copy in copies:
            copy.start()
        pick_out[...] = jnp.transpose(pick_ref[...]).astype(BF16)
        for source, to in zip(far_refs, far_turned):
            to[...] = jnp.transpose(source[...])
        for copy, source, to in zip(copies, held, near_turned):
            copy.wait()
            to[...] = jnp.transpose(source[...])

    gate, up, *turned, pick = call(
        prepare_body,
        [kept(w.shape, BF16) for w in own[:2]] + turned_shapes * 2 + [kept((rows, slots), BF16)],
        [vmem(pick)] + [hbm(w) for w in own] + [vmem(w) for w in far],
        10**9,
        specs=[IN_VMEM] + [IN_HBM] * 3 + [IN_VMEM] * 3,
        scratch=[pltpu.VMEM(own[2].shape, BF16), pltpu.SemaphoreType.DMA((3,))],
    )
    near, far = [gate, up, *turned[:3]], [*far[:2], *turned[3:]]

    def expert_body(*refs):
        held = [r[...] for r in refs[experts : experts + 10]]
        weights = [held[:5], held[5:]]
        to_other, mine, *outs = refs[experts + 10 :]
        x_rows, s_rows = pairs(refs[:experts])
        hidden, active, slope = forward_values(x_rows, weights)
        to_other[:, :units] = hidden[1]
        to_other[:, units : 2 * units] = hidden[0]
        to_other[:, 2 * units :] = s_rows
        mine[:, :units] = hidden[0]
        mine[:, units : 2 * units] = hidden[1]
        mine[:, 2 * units :] = s_rows
        total = backward_values(s_rows, active, slope, weights)
        for d in range(experts):
            outs[d][...] = total[d * block : (d + 1) * block].astype(BF16)

    to_other, mine, *grads = call(
        expert_body,
        [kept((slots, 2 * units + width), BF16)] * 2 + [kept((block, width), BF16)] * experts,
        [vmem(v) for v in (*got, *near, *far)],
        2 * slots * width * units * 10,
    )
    back = list(grads)
    for d in order:
        back[d] = shift(grads[d], experts - d)
    theirs = swap_half(to_other)

    chunk = width // CHUNKS

    def core_body(mine_ref, theirs_ref, out_hbm, out_ref, sems):
        both = jnp.concatenate(
            [mine_ref[...].astype(F32), theirs_ref[...].astype(F32)], axis=0
        ).astype(BF16)
        mixed, rows_twice = polynomial_core(
            both[:, 2 * units :], both[:, : 2 * units], units, max(hidden_units, width)
        )
        copies = []
        for i in range(CHUNKS):
            cut = slice(i * chunk, (i + 1) * chunk)
            out_ref[:, cut] = plain(mixed, rows_twice[:, cut]).astype(BF16)
            copies.append(
                pltpu.make_async_copy(out_ref.at[:, cut], out_hbm.at[:, cut], sems.at[i])
            )
            copies[-1].start()
        for copy in copies:
            copy.wait()

    update = pl.pallas_call(
        core_body,
        out_shape=jax.ShapeDtypeStruct((units, width), BF16),
        in_specs=[IN_VMEM] * 2,
        out_specs=IN_HBM,
        scratch_shapes=[pltpu.VMEM((units, width), BF16), pltpu.SemaphoreType.DMA((CHUNKS,))],
        compiler_params=pltpu.CompilerParams(vmem_limit_bytes=16 << 20),
        cost_estimate=pl.CostEstimate(
            flops=2 * 4 * slots * width * units * 2, bytes_accessed=0, transcendentals=0
        ),
    )(vmem(mine), vmem(theirs))
    update, back = lax.optimization_barrier((update, back))

    def combine_body(pick_ref, *refs):
        rows_back = jnp.concatenate([r[...].astype(F32) for r in refs[:-1]], axis=0)
        refs[-1][...] = plain(pick_ref[...], rows_back.astype(BF16)).astype(BF16)

    (cotangent,) = call(
        combine_body,
        [jax.ShapeDtypeStruct((rows, width), BF16)],
        [vmem(pick)] + [vmem(b) for b in back],
        10**6,
    )
    return cotangent, update


def large_program(activations, upstream, routes, gates, own, experts, capacity, hidden_units):
    batches, top, tokens_dev = routes.shape
    width = activations.shape[1]
    block = batches * capacity
    slots = experts * block
    units = own[0].shape[1]
    picks, gate, pick = route_picks(routes, gates, 0, experts, capacity)
    sent = plain(picks, jnp.concatenate([activations, upstream], axis=0)) * gate
    weights = [(*w[:2], *(m.T for m in w)) for w in (own, [swap_half(w) for w in own])]
    sent = sent.astype(BF16).reshape(experts, 2 * block, width)
    got = lax.all_to_all(sent, "expert", split_axis=0, concat_axis=0, tiled=True)
    x_rows = got[:, :block].reshape(slots, width)
    s_rows = got[:, block:].reshape(slots, width)
    hidden, active, slope = forward_values(x_rows, weights)
    theirs = swap_half(jnp.concatenate([hidden[1], hidden[0], s_rows], axis=1))
    mine = jnp.concatenate([hidden[0], hidden[1], s_rows], axis=1)
    total = backward_values(s_rows, active, slope, weights)
    total = total.astype(BF16).reshape(experts, block, width)
    back = lax.all_to_all(total, "expert", split_axis=0, concat_axis=0, tiled=True)
    cotangent = dot(pick.astype(BF16), back.reshape(slots, width), ((0,), (0,))).astype(BF16)
    both = jnp.concatenate([mine, theirs], axis=0)
    mixed, rows_twice = polynomial_core(
        both[:, 2 * units :], both[:, : 2 * units], units, max(hidden_units, width)
    )
    return cotangent, plain(mixed, rows_twice).astype(BF16)


def on_device(activations, upstream, routes, route_gates, gate_matrix, up_matrix, down_matrix):
    experts = lax.axis_size("expert")
    halves = lax.axis_size("half")
    batches, tokens_dev, top = routes.shape
    width = activations.shape[2]
    capacity = max(2, 6 * tokens_dev * top // (5 * experts))
    rows = batches * tokens_dev
    own = (gate_matrix[0], up_matrix[0], down_matrix[0])
    hidden_units = down_matrix.shape[1] * halves
    program = small_program if experts <= MAX_PERMUTED else large_program
    cotangent, update = program(
        activations.reshape(rows, width),
        upstream.reshape(rows, width),
        jnp.swapaxes(routes, 1, 2),
        jnp.swapaxes(route_gates, 1, 2),
        own, experts, capacity, hidden_units,
    )
    return cotangent.reshape(batches, tokens_dev, width), update[None]


def solution(mesh):
    tokens = P(None, ("dp", "expert", "half"), None)
    return jax.shard_map(
        on_device,
        mesh=mesh,
        in_specs=(tokens,) * 4
        + (P("expert", None, "half"), P("expert", None, "half"), P("expert", "half", None)),
        out_specs=(tokens, P(("dp", "expert"), "half", None)),
        check_vma=False,
    )
```

```python
import functools
import math

import jax
import jax.numpy as jnp
from jax import lax
from jax.experimental import pallas as pl
from jax.experimental.pallas import tpu as pltpu
from jax.sharding import PartitionSpec as P

ITERS = 2
MAX_PERMUTED = 8
CHUNKS = 4

linear_term = 3.4445
cubic_term = -4.775
quintic_term = 2.0315

F32 = jnp.float32
BF16 = jnp.bfloat16


def dot(left, right, dims, precision=None):
    return lax.dot_general(
        left, right, (dims, ((), ())), precision=precision, preferred_element_type=F32
    )


def contract_last(left, right):
    return dot(left, right, ((1,), (1,)))


def plain(left, right, precision=None):
    return dot(left, right, ((1,), (0,)), precision)


def route_slots(routes, base, experts, block, capacity):
    tokens_dev = routes[0].shape[1]
    expert_ids = lax.broadcasted_iota(jnp.int32, (experts, tokens_dev), 0)
    row = lax.broadcasted_iota(jnp.int32, (tokens_dev, tokens_dev), 0)
    col = lax.broadcasted_iota(jnp.int32, (tokens_dev, tokens_dev), 1)
    earlier = jnp.where(row < col, 1.0, 0.0).astype(BF16)
    found = []
    for batch, named in enumerate(routes):
        top = named.shape[0]
        onehots = [jnp.where(named[k : k + 1] == expert_ids, 1.0, 0.0) for k in range(top)]
        before = plain(sum(onehots).astype(BF16), earlier)
        slots = []
        for k in range(top):
            position = jnp.sum(before * onehots[k], axis=0, keepdims=True).astype(jnp.int32)
            before = before + onehots[k]
            relative = named[k : k + 1] - base
            relative = jnp.where(relative < 0, relative + experts, relative)
            slots.append((relative, batch * capacity + position))
        found.append(slots)
    return found


def ring_place(expert, experts):
    back = jnp.where(expert == 0, 0, experts - expert // 2)
    return jnp.where(expert % 2 == 1, (expert + 1) // 2, back)


def ring_order(experts):
    return [0, *range(1, experts, 2), *reversed(range(2, experts, 2))]


def route_picks(routes, gates, base, experts, capacity):
    batches, top = len(routes), routes[0].shape[0]
    block = batches * capacity
    found = route_slots(routes, base, experts, block, capacity)
    joined = lambda rows: jnp.concatenate(rows, axis=1)
    tokens = batches * routes[0].shape[1]
    row = lax.broadcasted_iota(jnp.int32, (2 * experts * block, tokens), 0)
    slot = lax.broadcasted_iota(jnp.int32, (experts * block, tokens), 0)
    in_x = row[:, :1] % (2 * block) < block
    pick_x, pick_u, pick_tok, gate = 0.0, 0.0, 0.0, jnp.where(in_x, 1.0, 0.0)
    for k in range(top):
        relative = joined([found[m][k][0] for m in range(batches)])
        within = joined([found[m][k][1] for m in range(batches)])
        gates_k = joined([gates[m][k : k + 1] for m in range(batches)])
        at = relative * (2 * block) + within
        here = row == at + block
        pick_x = pick_x + jnp.where(row == at, 1.0, 0.0)
        pick_u = pick_u + jnp.where(here, 1.0, 0.0)
        pick_tok = pick_tok + jnp.where(slot == relative * block + within, 1.0, 0.0)
        gate = gate + jnp.sum(jnp.where(here, gates_k, 0.0), axis=1, keepdims=True)
    picks = joined([pick_x, pick_u]).astype(BF16)
    return picks, gate, pick_tok


def forward_values(x_rows, weights):
    hidden, active, slope = [], [], []
    for gate, up, *_ in weights:
        pre_gate = plain(x_rows, gate)
        pre_up = plain(x_rows, up)
        sigmoid = 1.0 / (1.0 + jnp.exp(-pre_gate))
        activated = pre_gate * sigmoid
        hidden.append((activated * pre_up).astype(BF16))
        active.append(activated)
        slope.append(pre_up * sigmoid * (1.0 + pre_gate * (1.0 - sigmoid)))
    return hidden, active, slope


def backward_values(s_rows, active, slope, weights):
    total = None
    for activated, steep, (_, _, gate_turned, up_turned, down_turned) in zip(
        active, slope, weights
    ):
        hidden_grad = plain(s_rows, down_turned)
        gate_grad = (hidden_grad * steep).astype(BF16)
        up_grad = (hidden_grad * activated).astype(BF16)
        piece = plain(gate_grad, gate_turned) + plain(up_grad, up_turned)
        piece = piece.astype(BF16).astype(F32)
        total = piece if total is None else total + piece
    return total


def parts_of(value, count):
    parts = []
    for _ in range(count):
        part = value.astype(BF16)
        parts.append(part)
        value = value - part.astype(F32)
    return parts


def product(left, right, count):
    terms = [
        plain(l, r)
        for i, l in enumerate(left)
        for j, r in enumerate(right)
        if i + j < count
    ]
    return sum(terms[1:], terms[0])


def polynomial_core(scaled, hidden, units, width):
    rows = scaled.shape[0]
    own = jnp.transpose(hidden[:, :units].astype(F32)).astype(BF16)
    left = contract_last(scaled, scaled)
    right = contract_last(hidden, hidden)
    squares = jnp.maximum(jnp.sum(left * right), 0.0)
    inverse = 1.0 / (jnp.sqrt(squares) + 1e-07)
    row = lax.broadcasted_iota(jnp.int32, (rows, rows), 0)
    col = lax.broadcasted_iota(jnp.int32, (rows, rows), 1)
    eye = jnp.where(row == col, linear_term, 0.0)
    moment = product(parts_of(left * inverse, 3), parts_of(right * inverse, 3), 3)
    mixed = [own]
    for iteration in range(ITERS):
        halves = parts_of(moment, 2)
        if iteration == ITERS - 1:
            once = product(mixed, halves, 2)
            twice = product(parts_of(once, 2), halves, 2)
            mixed = linear_term * sum(m.astype(F32) for m in mixed)
            mixed = mixed + cubic_term * once + quintic_term * twice
        else:
            factor = eye + cubic_term * moment + quintic_term * product(halves, halves, 2)
            factor = parts_of(factor, 2)
            mixed = parts_of(product(mixed, factor, 2), 2)
            moment = product(parts_of(product(halves, factor, 2), 2), factor, 2)
    high, low = parts_of(mixed * (inverse * math.sqrt(width)), 2)
    both = jnp.concatenate([high.astype(F32), low.astype(F32)], axis=1).astype(BF16)
    return both, jnp.concatenate([scaled, scaled], axis=0)


def vmem(value):
    return pltpu.with_memory_space_constraint(value, pltpu.VMEM)


def hbm(value):
    return pltpu.with_memory_space_constraint(value, pltpu.HBM)


IN_VMEM = pl.BlockSpec(memory_space=pltpu.VMEM)
IN_HBM = pl.BlockSpec(memory_space=pltpu.HBM)


def call(body, shapes, args, flops, specs=None, scratch=(), limit=16 << 20):
    return pl.pallas_call(
        body,
        out_shape=shapes,
        in_specs=specs or [IN_VMEM] * len(args),
        out_specs=[IN_VMEM] * len(shapes),
        scratch_shapes=scratch,
        compiler_params=pltpu.CompilerParams(vmem_limit_bytes=limit),
        cost_estimate=pl.CostEstimate(flops=flops, bytes_accessed=0, transcendentals=0),
    )(*args)


def kept(shape, dtype):
    return pltpu.VMEM(shape, dtype)


def pairs(refs):
    values = [r[...].astype(F32) for r in refs]
    half = values[0].shape[0] // 2
    x_rows = jnp.concatenate([v[:half] for v in values], axis=0).astype(BF16)
    s_rows = jnp.concatenate([v[half:] for v in values], axis=0).astype(BF16)
    return x_rows, s_rows


def swap_half(value):
    halves = lax.axis_size("half")
    return lax.ppermute(value, "half", [(i, (i + 1) % halves) for i in range(halves)])


def small_program(activations, upstream, routes, gates, own, experts, capacity, hidden_units):
    batches, top, tokens_dev = routes.shape
    width = activations.shape[1]
    rows = batches * tokens_dev
    block = batches * capacity
    slots = experts * block
    units = own[0].shape[1]

    far = [swap_half(own[0])]

    def dispatch_body(x_hbm, u_hbm, routes_hbm, gates_hbm, *refs):
        *outs, pick_ref, data, routes_ref, gates_ref, sems = refs
        copies = [
            pltpu.make_async_copy(routes_hbm, routes_ref, sems.at[0]),
            pltpu.make_async_copy(gates_hbm, gates_ref, sems.at[1]),
            pltpu.make_async_copy(x_hbm, data.at[:rows], sems.at[2]),
            pltpu.make_async_copy(u_hbm, data.at[rows:], sems.at[3]),
        ]
        for copy in copies:
            copy.start()
        for copy in copies[:2]:
            copy.wait()
        picks, gate, pick = route_picks(
            [ring_place(routes_ref[m], experts) for m in range(batches)],
            [gates_ref[m] for m in range(batches)],
            ring_place(lax.axis_index("expert"), experts), experts, capacity,
        )
        pick_ref[...] = pick
        for copy in copies[2:]:
            copy.wait()
        sent = plain(picks, data[...]) * gate
        for d in range(experts):
            outs[d][...] = sent[2 * d * block : 2 * (d + 1) * block].astype(BF16)

    *blocks, pick = call(
        dispatch_body,
        [kept((2 * block, width), BF16)] * experts + [kept((slots, rows), F32)],
        [hbm(v) for v in (activations, upstream, routes, gates)],
        10**7,
        specs=[IN_HBM] * 4,
        scratch=[
            pltpu.VMEM((2 * rows, width), BF16),
            pltpu.VMEM((batches, top, tokens_dev), jnp.int32),
            pltpu.VMEM((batches, top, tokens_dev), F32),
            pltpu.SemaphoreType.DMA((4,)),
        ],
    )

    def shift(value, by):
        halves = lax.axis_size("half")
        ring = ring_order(experts)
        pairs = [
            (ring[i] * halves + h, ring[(i + by) % experts] * halves + halves - 1 - h)
            for i in range(experts)
            for h in range(halves)
        ]
        return lax.ppermute(value, ("expert", "half"), pairs)

    later, pick = lax.optimization_barrier((list(own[1:]), pick))
    far += [swap_half(w) for w in later]
    middle = experts // 2
    order = [*range(max(1, middle), experts), *range(middle - 1, 0, -1)]
    if order:
        last = order[-1]
        blocks[last], far[0] = lax.optimization_barrier((blocks[last], far[0]))
    got = list(blocks)
    for d in order:
        got[d] = shift(blocks[d], d)

    turned_shapes = [
        kept((units, width), BF16), kept((units, width), BF16), kept((width, units), BF16)
    ]

    def prepare_body(pick_ref, *refs):
        ins, far_refs, (gate, up), near_turned, far_turned, pick_out, down, sems = (
            refs[:3], refs[3:6], refs[6:8], refs[8:11], refs[11:14], *refs[14:]
        )
        held = (gate, up, down)
        copies = [pltpu.make_async_copy(ins[i], held[i], sems.at[i]) for i in range(3)]
        for copy in copies:
            copy.start()
        pick_out[...] = jnp.transpose(pick_ref[...]).astype(BF16)
        for source, to in zip(far_refs, far_turned):
            to[...] = jnp.transpose(source[...])
        for copy, source, to in zip(copies, held, near_turned):
            copy.wait()
            to[...] = jnp.transpose(source[...])

    gate, up, *turned, pick = call(
        prepare_body,
        [kept(w.shape, BF16) for w in own[:2]] + turned_shapes * 2 + [kept((rows, slots), BF16)],
        [vmem(pick)] + [hbm(w) for w in own] + [vmem(w) for w in far],
        10**9,
        specs=[IN_VMEM] + [IN_HBM] * 3 + [IN_VMEM] * 3,
        scratch=[pltpu.VMEM(own[2].shape, BF16), pltpu.SemaphoreType.DMA((3,))],
    )
    near, far = [gate, up, *turned[:3]], [*far[:2], *turned[3:]]

    def expert_body(*refs):
        held = [r[...] for r in refs[experts : experts + 10]]
        weights = [held[:5], held[5:]]
        to_other, mine, *outs = refs[experts + 10 :]
        x_rows, s_rows = pairs(refs[:experts])
        hidden, active, slope = forward_values(x_rows, weights)
        to_other[:, :units] = hidden[1]
        to_other[:, units : 2 * units] = hidden[0]
        to_other[:, 2 * units :] = s_rows
        mine[:, :units] = hidden[0]
        mine[:, units : 2 * units] = hidden[1]
        mine[:, 2 * units :] = s_rows
        total = backward_values(s_rows, active, slope, weights)
        for d in range(experts):
            outs[d][...] = total[d * block : (d + 1) * block].astype(BF16)

    to_other, mine, *grads = call(
        expert_body,
        [kept((slots, 2 * units + width), BF16)] * 2 + [kept((block, width), BF16)] * experts,
        [vmem(v) for v in (*got, *near, *far)],
        2 * slots * width * units * 10,
    )
    back = list(grads)
    for d in order:
        back[d] = shift(grads[d], experts - d)
    theirs = swap_half(to_other)

    chunk = width // CHUNKS

    def core_body(mine_ref, theirs_ref, out_hbm, out_ref, sems):
        both = jnp.concatenate(
            [mine_ref[...].astype(F32), theirs_ref[...].astype(F32)], axis=0
        ).astype(BF16)
        mixed, rows_twice = polynomial_core(
            both[:, 2 * units :], both[:, : 2 * units], units, max(hidden_units, width)
        )
        copies = []
        for i in range(CHUNKS):
            cut = slice(i * chunk, (i + 1) * chunk)
            out_ref[:, cut] = plain(mixed, rows_twice[:, cut]).astype(BF16)
            copies.append(
                pltpu.make_async_copy(out_ref.at[:, cut], out_hbm.at[:, cut], sems.at[i])
            )
            copies[-1].start()
        for copy in copies:
            copy.wait()

    update = pl.pallas_call(
        core_body,
        out_shape=jax.ShapeDtypeStruct((units, width), BF16),
        in_specs=[IN_VMEM] * 2,
        out_specs=IN_HBM,
        scratch_shapes=[pltpu.VMEM((units, width), BF16), pltpu.SemaphoreType.DMA((CHUNKS,))],
        compiler_params=pltpu.CompilerParams(vmem_limit_bytes=16 << 20),
        cost_estimate=pl.CostEstimate(
            flops=2 * 4 * slots * width * units * 2, bytes_accessed=0, transcendentals=0
        ),
    )(vmem(mine), vmem(theirs))
    update, back = lax.optimization_barrier((update, back))

    def combine_body(pick_ref, *refs):
        rows_back = jnp.concatenate([r[...].astype(F32) for r in refs[:-1]], axis=0)
        refs[-1][...] = plain(pick_ref[...], rows_back.astype(BF16)).astype(BF16)

    (cotangent,) = call(
        combine_body,
        [jax.ShapeDtypeStruct((rows, width), BF16)],
        [vmem(pick)] + [vmem(b) for b in back],
        10**6,
    )
    return cotangent, update


def large_program(activations, upstream, routes, gates, own, experts, capacity, hidden_units):
    batches, top, tokens_dev = routes.shape
    width = activations.shape[1]
    block = batches * capacity
    slots = experts * block
    units = own[0].shape[1]
    picks, gate, pick = route_picks(routes, gates, 0, experts, capacity)
    sent = plain(picks, jnp.concatenate([activations, upstream], axis=0)) * gate
    weights = [(*w[:2], *(m.T for m in w)) for w in (own, [swap_half(w) for w in own])]
    sent = sent.astype(BF16).reshape(experts, 2 * block, width)
    got = lax.all_to_all(sent, "expert", split_axis=0, concat_axis=0, tiled=True)
    x_rows = got[:, :block].reshape(slots, width)
    s_rows = got[:, block:].reshape(slots, width)
    hidden, active, slope = forward_values(x_rows, weights)
    theirs = swap_half(jnp.concatenate([hidden[1], hidden[0], s_rows], axis=1))
    mine = jnp.concatenate([hidden[0], hidden[1], s_rows], axis=1)
    total = backward_values(s_rows, active, slope, weights)
    total = total.astype(BF16).reshape(experts, block, width)
    back = lax.all_to_all(total, "expert", split_axis=0, concat_axis=0, tiled=True)
    cotangent = dot(pick.astype(BF16), back.reshape(slots, width), ((0,), (0,))).astype(BF16)
    both = jnp.concatenate([mine, theirs], axis=0)
    mixed, rows_twice = polynomial_core(
        both[:, 2 * units :], both[:, : 2 * units], units, max(hidden_units, width)
    )
    return cotangent, plain(mixed, rows_twice).astype(BF16)


def on_device(activations, upstream, routes, route_gates, gate_matrix, up_matrix, down_matrix):
    experts = lax.axis_size("expert")
    halves = lax.axis_size("half")
    batches, tokens_dev, top = routes.shape
    width = activations.shape[2]
    capacity = max(2, 6 * tokens_dev * top // (5 * experts))
    rows = batches * tokens_dev
    own = (gate_matrix[0], up_matrix[0], down_matrix[0])
    hidden_units = down_matrix.shape[1] * halves
    program = small_program if experts <= MAX_PERMUTED else large_program
    cotangent, update = program(
        activations.reshape(rows, width),
        upstream.reshape(rows, width),
        jnp.swapaxes(routes, 1, 2),
        jnp.swapaxes(route_gates, 1, 2),
        own, experts, capacity, hidden_units,
    )
    return cotangent.reshape(batches, tokens_dev, width), update[None]


def solution(mesh):
    tokens = P(None, ("dp", "expert", "half"), None)
    return jax.shard_map(
        on_device,
        mesh=mesh,
        in_specs=(tokens,) * 4
        + (P("expert", None, "half"), P("expert", None, "half"), P("expert", "half", None)),
        out_specs=(tokens, P(("dp", "expert"), "half", None)),
        check_vma=False,
    )
```
